128 devices in a mesh: blk: 32 (over x, z_lo, y), uly: 4 (over z_hi, core).
Axes of the slice: x: 4, y: 4, z: 4 (z_hi: 2, z_lo: 2; z = z_hi * 2 + z_lo), core: 2. Of those that a mesh axis runs over, the one named last changes fastest.
Arguments:
- queries: bfloat16 [10240, 2560], P(('blk', 'uly')), may hold values from -17 to 17
- keys: bfloat16 [10240, 2560], P(('blk', 'uly')), may hold values from -8 to 8
- values: bfloat16 [10240, 2560], P(('blk', 'uly')), may hold values from -2.5 to 2.5
Outputs:
- attended: bfloat16 [10240, 2560], P(('blk', 'uly'))
The draws below stay inside these ranges and needn't reach their ends.
All inputs are finite; a program needn't handle non-finite values.
Results may differ from the reference program's by a relative error of at most 0.00665.
Values may be sent and summed in bfloat16 or wider, within the bound.
No kernel may reach another device: no remote copies, remote signals or barrier semaphores. Data moves between devices by JAX's collectives and lax.ppermute only.
A program may use at most 128 MiB of HBM per device.

```python
import jax
import jax.numpy as jnp
from jax import lax

HEADS = 20
HEAD_DIM = 128
SEQ = 10240


def draw_keys(key, part):
    key = jax.random.fold_in(key, 2)
    return (2.0 * jnp.clip(jax.random.normal(key, (SEQ, HEADS * HEAD_DIM), jnp.float32), -4.0, 4.0)).astype(jnp.bfloat16)


def draw_queries(key, part):
    key = jax.random.fold_in(key, 5)
    return (1.5 * jnp.clip(jax.random.normal(key, (SEQ, HEADS * HEAD_DIM), jnp.float32), -4.0, 4.0)).astype(jnp.bfloat16)


def shard_levels(own_key, extent, shards, low, largest):
    level = 1.0
    for position, parts in shards:
        heights = jax.random.uniform(jax.random.fold_in(jax.random.fold_in(own_key, 6), position), (parts,), jnp.float32, low / len(shards), largest / len(shards))
        level = level * jnp.repeat(jnp.exp(heights), extent[position] // parts).reshape((-1,) + (1,) * (len(extent) - 1 - position))
    return level


def gaussian(stream_key, dims, deviation, bound, pieces=(), dtype=jnp.bfloat16):
    values = jax.random.normal(stream_key, dims, jnp.float32) * deviation
    if len(pieces) > 0:
        values = shard_levels(stream_key, dims, pieces, -0.22, 0.18) * values
    return jnp.clip(values, min=-bound, max=bound).astype(dtype)


def setup_inputs(seed: int = 0) -> dict:
    key_list = jax.random.split(jax.random.key(seed), 4)
    return {
        "queries": draw_queries(jax.random.fold_in(key_list[3], 71), 0),
        "keys": draw_keys(jax.random.fold_in(key_list[3], 71), 0),
        "values": gaussian(key_list[2], (SEQ, HEADS * HEAD_DIM), 0.4, 2.5, ((0, 128),)),
    }


def divisor_upto(total, cap):
    best = 1
    for cand in range(1, min(total, cap) + 1):
        if total % cand == 0:
            best = cand
    return best


def head_attention(query_head, key_head, value_head):
    block = divisor_upto(SEQ, 2048)
    scale = float(HEAD_DIM) ** -0.5
    query_blocks = query_head.reshape(SEQ // block, block, HEAD_DIM)

    def one_block(query_block):
        scores = jnp.dot(query_block, key_head.T, preferred_element_type=jnp.float32) * scale
        top = jnp.max(scores, axis=-1, keepdims=True)
        weights = jnp.exp(scores - top)
        total = jnp.sum(weights, axis=-1, keepdims=True)
        summed = jnp.dot(weights.astype(jnp.bfloat16), value_head, preferred_element_type=jnp.float32)
        return (summed / total).astype(jnp.bfloat16)

    return lax.map(one_block, query_blocks).reshape(SEQ, HEAD_DIM)


def reference(queries, keys, values):
    def split_heads(array):
        return array.reshape(SEQ, HEADS, HEAD_DIM).transpose(1, 0, 2)

    per_head = lax.map(lambda group: head_attention(group[0], group[1], group[2]),
                       (split_heads(queries), split_heads(keys), split_heads(values)))
    return per_head.transpose(1, 0, 2).reshape(SEQ, HEADS * HEAD_DIM)
```

```python
import functools

import jax
import jax.numpy as jnp
from jax import lax
from jax.experimental import pallas as pl
from jax.experimental.pallas import tpu as pltpu
from jax.sharding import Mesh, PartitionSpec as P

HEADS = 20
HEAD_DIM = 128
SCALE = HEAD_DIM**-0.5 * 1.4426950408889634
AXES = ("x", "zl", "y", "zh", "c")
SIZES = (4, 2, 4, 2, 2)
DEVICES = 128
SHARE = 6
Q_ROWS = 14
KV_ROWS = 40
NT = (((1,), (1,)), ((), ()))


def scaled_halves(q):
    full = q.astype(jnp.float32) * SCALE
    high = full.astype(jnp.bfloat16)
    low = (full - high.astype(jnp.float32)).astype(jnp.bfloat16)
    return jnp.concatenate([high, low], axis=1)


def attend_kernel(q_block, k_block, first, last, *refs):
    refs = list(refs)
    q_ref, kv_ref = refs[:2]
    refs = refs[2:]
    if not first:
        acc_in, top_in = refs[:2]
        refs = refs[2:]
    rows, keys = q_ref.shape[0], kv_ref.shape[0]
    ones = jnp.ones((k_block, HEAD_DIM), jnp.bfloat16)
    for i in range(rows // q_block):
        here = slice(i * q_block, (i + 1) * q_block)
        q = scaled_halves(q_ref[here, :])
        if first:
            top = jnp.full((q_block, 1), -1e30, jnp.float32)
            acc = jnp.zeros((q_block, 2 * HEAD_DIM), jnp.float32)
        else:
            top = top_in[here, :1]
            acc = acc_in[here, :]
        for j in range(keys // k_block):
            there = slice(j * k_block, (j + 1) * k_block)
            k = kv_ref[there, :HEAD_DIM]
            v = kv_ref[there, HEAD_DIM:]
            scores = lax.dot_general(
                q, jnp.concatenate([k, k], axis=1), NT, preferred_element_type=jnp.float32
            )
            fresh = jnp.maximum(top, jnp.max(scores, axis=1, keepdims=True))
            weights = jnp.exp2(scores - fresh).astype(jnp.bfloat16)
            acc = acc * jnp.exp2(top - fresh) + jnp.dot(
                weights, jnp.concatenate([v, ones], axis=1), preferred_element_type=jnp.float32
            )
            top = fresh
        if last:
            refs[0][here, :] = (acc[:, :HEAD_DIM] / acc[:, HEAD_DIM:]).astype(jnp.bfloat16)
        else:
            refs[0][here, :] = acc
            refs[1][here, :] = jnp.broadcast_to(top, (q_block, HEAD_DIM))


def attend(q, kv, state, last, q_block=896, k_block=512):
    rows, keys = q.shape[0], kv.shape[0]
    first = state is None
    if last:
        out_shape = (jax.ShapeDtypeStruct((rows, HEAD_DIM), jnp.bfloat16),)
    else:
        out_shape = (
            jax.ShapeDtypeStruct((rows, 2 * HEAD_DIM), jnp.float32),
            jax.ShapeDtypeStruct((rows, HEAD_DIM), jnp.float32),
        )
    args = (q, kv) + (() if first else state)
    return pl.pallas_call(
        functools.partial(attend_kernel, q_block, k_block, first, last),
        out_shape=out_shape,
        in_specs=[pl.BlockSpec(memory_space=pltpu.VMEM)] * len(args),
        out_specs=tuple(pl.BlockSpec(memory_space=pltpu.VMEM) for _ in out_shape),
        compiler_params=pltpu.CompilerParams(vmem_limit_bytes=48 * 2**20),
        cost_estimate=pl.CostEstimate(
            flops=8 * rows * keys * HEAD_DIM, bytes_accessed=4 * keys * HEAD_DIM, transcendentals=rows * keys
        ),
    )(*args)


def local(queries, keys, values):
    tokens = queries.shape[0]
    spare = DEVICES - HEADS * SHARE
    queries = queries.reshape(tokens, HEADS, HEAD_DIM)
    keys = keys.reshape(tokens, HEADS, HEAD_DIM)
    values = values.reshape(tokens, HEADS, HEAD_DIM)
    q = jnp.pad(queries, ((0, SHARE * Q_ROWS - tokens), (0, 0), (0, 0)))
    q = q.reshape(SHARE, 2, Q_ROWS // 2, HEADS, HEAD_DIM).transpose(3, 0, 2, 1, 4)
    q = q.reshape(HEADS * SHARE, Q_ROWS // 2, 2 * HEAD_DIM)
    kv = jnp.concatenate([keys, values], axis=-1)
    kv = kv.reshape(2, KV_ROWS, HEADS, 2 * HEAD_DIM).transpose(2, 0, 1, 3)
    kv = jnp.broadcast_to(kv[:, None], (HEADS, SHARE // 2, 2, KV_ROWS, 2 * HEAD_DIM))
    kv = kv.reshape(HEADS * SHARE, KV_ROWS, 2 * HEAD_DIM)
    sent = jnp.concatenate([jnp.pad(q, ((0, 0), (0, 1), (0, 0))), kv], axis=1)
    sent = jnp.pad(sent, ((0, spare), (0, 0), (0, 0)))
    got = lax.all_to_all(sent, AXES, 0, 0, tiled=True)
    q = got[:, : Q_ROWS // 2].reshape(DEVICES, Q_ROWS // 2, 2, HEAD_DIM).transpose(2, 0, 1, 3)
    q = q.reshape(DEVICES * Q_ROWS, HEAD_DIM)
    kv = got[:, 8:].reshape(DEVICES * KV_ROWS, 2 * HEAD_DIM)
    other = lax.ppermute(kv, "c", [(0, 1), (1, 0)])
    state = attend(q, kv, None, False)
    (out,) = attend(q, other, state, True)
    out = out.reshape(2, DEVICES, Q_ROWS // 2, HEAD_DIM).transpose(1, 2, 0, 3)
    out = out.reshape(DEVICES, Q_ROWS // 2, 2 * HEAD_DIM)
    back = lax.all_to_all(out, AXES, 0, 0, tiled=True)[: HEADS * SHARE]
    back = back.reshape(HEADS, SHARE, Q_ROWS // 2, 2, HEAD_DIM).transpose(1, 3, 2, 0, 4)
    return back.reshape(SHARE * Q_ROWS, HEADS * HEAD_DIM)[:tokens]


def solution(mesh):
    fine = Mesh(mesh.devices.reshape(SIZES), AXES)
    return jax.shard_map(
        local, mesh=fine, in_specs=(P(AXES, None),) * 3, out_specs=P(AXES, None), check_vma=False
    )
```

```python
import functools

import jax
import jax.numpy as jnp
from jax import lax
from jax.experimental import pallas as pl
from jax.experimental.pallas import tpu as pltpu
from jax.sharding import Mesh, PartitionSpec as P

HEADS = 20
HEAD_DIM = 128
PAIR = 2 * HEAD_DIM
SCALE = HEAD_DIM**-0.5 * 1.4426950408889634
AXES = ("x", "zl", "y", "zh", "c")
SIZES = (4, 2, 4, 2, 2)
COLUMNS = 16
TOKENS = 80
QUARTER = TOKENS // 4
NT = (((1,), (1,)), ((), ()))
KV_ROWS, Q_ROWS, XKV_ROWS, XQ_ROWS = TOKENS, TOKENS // 2, QUARTER, QUARTER // 2
VMEM = pl.BlockSpec(memory_space=pltpu.VMEM)


def along_z(a, step):
    pairs = []
    for zl in range(2):
        for zh in range(2):
            z = (2 * zh + zl + step) % 4
            pairs.append((2 * zl + zh, 2 * (z % 2) + z // 2))
    return lax.ppermute(a, ("zl", "zh"), pairs)


def along_y(a, step):
    return lax.ppermute(a, "y", [(y, (y + step) % 4) for y in range(4)])


def other_core(a):
    return lax.ppermute(a, "c", [(0, 1), (1, 0)])


def scaled_halves(q):
    full = q.astype(jnp.float32) * SCALE
    high = full.astype(jnp.bfloat16)
    low = (full - high.astype(jnp.float32)).astype(jnp.bfloat16)
    return jnp.concatenate([high, low], axis=1)


def attend_kernel(k_block, n_kv, first, last, *refs):
    refs = list(refs)
    q_ref, kv_refs, refs = refs[0], refs[1 : 1 + n_kv], refs[1 + n_kv :]
    if not first:
        acc_in, top_in = refs[:2]
        refs = refs[2:]
    rows = q_ref.shape[0]
    ones = jnp.ones((k_block, HEAD_DIM), jnp.bfloat16)
    for half in range(2):
        lanes = slice(half * HEAD_DIM, (half + 1) * HEAD_DIM)
        here = slice(half * rows, (half + 1) * rows)
        q = scaled_halves(q_ref[:, lanes])
        if first:
            top = jnp.full((rows, 1), -1e30, jnp.float32)
            acc = jnp.zeros((rows, PAIR), jnp.float32)
        else:
            top = jnp.max(top_in[here, :], axis=1, keepdims=True)
            acc = acc_in[here, :]
        for kv_ref in kv_refs:
            for j in range(kv_ref.shape[0] // k_block):
                there = slice(j * k_block, (j + 1) * k_block)
                k = kv_ref[there, :HEAD_DIM]
                v = kv_ref[there, HEAD_DIM:]
                scores = lax.dot_general(
                    q, jnp.concatenate([k, k], axis=1), NT, preferred_element_type=jnp.float32
                )
                fresh = jnp.maximum(top, jnp.max(scores, axis=1, keepdims=True))
                weights = jnp.exp2(scores - fresh).astype(jnp.bfloat16)
                acc = acc * jnp.exp2(top - fresh) + jnp.dot(
                    weights, jnp.concatenate([v, ones], axis=1), preferred_element_type=jnp.float32
                )
                top = fresh
        if last == "out":
            refs[0][:, lanes] = (acc[:, :HEAD_DIM] / acc[:, HEAD_DIM:]).astype(jnp.bfloat16)
        elif last == "part":
            total = acc[:, HEAD_DIM:]
            refs[0][:, lanes] = (acc[:, :HEAD_DIM] / total).astype(jnp.bfloat16)
            level = top + jnp.log2(total)
            high = level.astype(jnp.bfloat16)
            rest = level - high.astype(jnp.float32)
            middle = rest.astype(jnp.bfloat16)
            low = (rest - middle.astype(jnp.float32)).astype(jnp.bfloat16)
            lane = lax.broadcasted_iota(jnp.int32, level.shape, 1)
            zero = jnp.zeros_like(level)
            coded = jnp.where(lane == 0, high.astype(jnp.float32), zero)
            coded = jnp.where(lane == 1, middle.astype(jnp.float32), coded)
            coded = jnp.where(lane == 2, low.astype(jnp.float32), coded)
            refs[0][:, PAIR + half * HEAD_DIM : PAIR + (half + 1) * HEAD_DIM] = coded.astype(jnp.bfloat16)
        else:
            refs[0][here, :] = acc
            refs[1][here, :] = jnp.broadcast_to(top, (rows, HEAD_DIM))


def attend(q, kvs, state, last, k_block=256):
    rows = q.shape[0]
    keys = sum(kv.shape[0] for kv in kvs)
    if last is None:
        out_shape = (
            jax.ShapeDtypeStruct((2 * rows, PAIR), jnp.float32),
            jax.ShapeDtypeStruct((2 * rows, HEAD_DIM), jnp.float32),
        )
    else:
        out_shape = (jax.ShapeDtypeStruct((rows, PAIR if last == "out" else 2 * PAIR), jnp.bfloat16),)
    args = (q, *kvs, *(state or ()))
    result = pl.pallas_call(
        functools.partial(attend_kernel, k_block, len(kvs), state is None, last),
        out_shape=out_shape,
        in_specs=[VMEM] * len(args),
        out_specs=(VMEM,) * len(out_shape),
        compiler_params=pltpu.CompilerParams(vmem_limit_bytes=40 * 2**20),
        cost_estimate=pl.CostEstimate(
            flops=16 * rows * keys * HEAD_DIM, bytes_accessed=4 * keys * HEAD_DIM, transcendentals=2 * rows * keys
        ),
    )(*args)
    return result if last is None else result[0]


def combine_kernel(*refs):
    parts, out = refs[:-1], refs[-1]
    for half in range(2):
        lanes = slice(half * HEAD_DIM, (half + 1) * HEAD_DIM)
        coded = slice(PAIR + half * HEAD_DIM, PAIR + (half + 1) * HEAD_DIM)
        levels = [jnp.sum(p[:, coded].astype(jnp.float32), axis=1, keepdims=True) for p in parts]
        top = functools.reduce(jnp.maximum, levels)
        shares = [jnp.exp2(level - top) for level in levels]
        total = functools.reduce(jnp.add, shares)
        summed = functools.reduce(
            jnp.add, [share * p[:, lanes].astype(jnp.float32) for share, p in zip(shares, parts, strict=True)]
        )
        out[:, lanes] = (summed / total).astype(jnp.bfloat16)


def combine(parts):
    rows = parts[0].shape[0]
    return pl.pallas_call(
        combine_kernel,
        out_shape=jax.ShapeDtypeStruct((rows, PAIR), jnp.bfloat16),
        in_specs=[VMEM] * len(parts),
        out_specs=VMEM,
        cost_estimate=pl.CostEstimate(flops=16 * rows * PAIR, bytes_accessed=16 * rows * PAIR, transcendentals=0),
    )(*parts)


def local(queries, keys, values):
    main = COLUMNS * HEAD_DIM
    extra_heads = HEADS - COLUMNS

    def by_column(a):
        return a[:, :main].reshape(TOKENS, COLUMNS, HEAD_DIM).transpose(1, 0, 2)

    def by_quarter(a):
        a = a[:, main:].reshape(4, QUARTER, extra_heads, HEAD_DIM).transpose(2, 0, 1, 3)
        return a.reshape(COLUMNS, QUARTER, HEAD_DIM)

    def paired(a):
        half = a.shape[1] // 2
        return jnp.concatenate([a[:, :half], a[:, half:]], axis=2)

    sent = jnp.concatenate(
        [
            jnp.concatenate([by_column(keys), by_column(values)], axis=2),
            paired(by_column(queries)),
            jnp.concatenate([by_quarter(keys), by_quarter(values)], axis=2),
            paired(by_quarter(queries)),
        ],
        axis=1,
    )
    got = lax.all_to_all(sent, ("x", "y"), 0, 0, tiled=True)

    def rows(start, count):
        return got[:, start : start + count].reshape(COLUMNS * count, PAIR)

    kv = rows(0, KV_ROWS)
    q = rows(KV_ROWS, Q_ROWS)
    xkv = rows(KV_ROWS + Q_ROWS, XKV_ROWS)
    xq = rows(KV_ROWS + Q_ROWS + XKV_ROWS, XQ_ROWS)

    xqs = [xq] + [along_z(xq, step) for step in (1, 3, 2)]
    xkvs = jnp.concatenate([xkv] + [along_y(xkv, step) for step in (1, 3, 2)], axis=0)
    kv_other = other_core(kv)
    kv_next, kv_before, kv_across = (along_z(kv, step) for step in (1, 3, 2))
    xkvs_other = other_core(xkvs)

    state = attend(q, [kv, kv_other], None, None)
    parts = attend(jnp.concatenate(xqs, axis=0), [xkvs, xkvs_other], None, "part")
    n = xq.shape[0]
    back = [parts[:n]] + [
        along_z(parts[i * n : (i + 1) * n], -step) for i, step in ((1, 1), (2, 3), (3, 2))
    ]
    xout = combine(back)
    state = attend(q, [kv_next, kv_before], state, None)
    state = attend(q, [other_core(kv_next), other_core(kv_before)], state, None)
    out = attend(q, [kv_across, other_core(kv_across)], state, "out")

    sent = jnp.concatenate(
        [out.reshape(COLUMNS, Q_ROWS, PAIR), xout.reshape(COLUMNS, XQ_ROWS, PAIR)], axis=1
    )
    got = lax.all_to_all(sent, ("x", "y"), 0, 0, tiled=True)
    out = got[:, :Q_ROWS].reshape(COLUMNS, Q_ROWS, 2, HEAD_DIM).transpose(2, 1, 0, 3).reshape(TOKENS, main)
    xout = got[:, Q_ROWS:].reshape(extra_heads, 4, XQ_ROWS, 2, HEAD_DIM).transpose(1, 3, 2, 0, 4)
    return jnp.concatenate([out, xout.reshape(TOKENS, extra_heads * HEAD_DIM)], axis=1)


def solution(mesh):
    fine = Mesh(mesh.devices.reshape(SIZES), AXES)
    return jax.shard_map(
        local, mesh=fine, in_specs=(P(AXES, None),) * 3, out_specs=P(AXES, None), check_vma=False
    )
```

```python
import functools

import jax
import jax.numpy as jnp
from jax import lax
from jax.experimental import pallas as pl
from jax.experimental.pallas import tpu as pltpu
from jax.sharding import Mesh, PartitionSpec as P

HEADS = 20
HEAD_DIM = 128
SCALE = HEAD_DIM**-0.5 * 1.4426950408889634
AXES = ("x", "zl", "y", "zh", "c")
SIZES = (4, 2, 4, 2, 2)
DEVICES = 128
SHARE = 6
Q_ROWS = 14
KV_ROWS = 40
NT = (((1,), (1,)), ((), ()))


def scaled_halves(q):
    full = q.astype(jnp.float32) * SCALE
    high = full.astype(jnp.bfloat16)
    low = (full - high.astype(jnp.float32)).astype(jnp.bfloat16)
    return jnp.concatenate([high, low], axis=1)


def attend_kernel(k_block, first, last, *refs):
    refs = list(refs)
    q_ref, kv_ref = refs[:2]
    refs = refs[2:]
    if not first:
        acc_in, top_in = refs[:2]
        refs = refs[2:]
    q_block, keys = q_ref.shape[0], kv_ref.shape[0]
    ones = jnp.ones((k_block, HEAD_DIM), jnp.bfloat16)
    for i in range(2):
        here = slice(i * q_block, (i + 1) * q_block)
        lanes = slice(i * HEAD_DIM, (i + 1) * HEAD_DIM)
        q = scaled_halves(q_ref[:, lanes])
        if first:
            top = jnp.full((q_block, 1), -1e30, jnp.float32)
            acc = jnp.zeros((q_block, 2 * HEAD_DIM), jnp.float32)
        else:
            top = jnp.max(top_in[here, :], axis=1, keepdims=True)
            acc = acc_in[here, :]
        for j in range(keys // k_block):
            there = slice(j * k_block, (j + 1) * k_block)
            k = kv_ref[there, :HEAD_DIM]
            v = kv_ref[there, HEAD_DIM:]
            scores = lax.dot_general(
                q, jnp.concatenate([k, k], axis=1), NT, preferred_element_type=jnp.float32
            )
            fresh = jnp.maximum(top, jnp.max(scores, axis=1, keepdims=True))
            weights = jnp.exp2(scores - fresh).astype(jnp.bfloat16)
            acc = acc * jnp.exp2(top - fresh) + jnp.dot(
                weights, jnp.concatenate([v, ones], axis=1), preferred_element_type=jnp.float32
            )
            top = fresh
        if last:
            refs[0][:, lanes] = (acc[:, :HEAD_DIM] / acc[:, HEAD_DIM:]).astype(jnp.bfloat16)
        else:
            refs[0][here, :] = acc
            refs[1][here, :] = jnp.broadcast_to(top, (q_block, HEAD_DIM))


def attend(q, kv, state, last, k_block=512):
    rows, keys = 2 * q.shape[0], kv.shape[0]
    first = state is None
    if last:
        out_shape = (jax.ShapeDtypeStruct(q.shape, jnp.bfloat16),)
    else:
        out_shape = (
            jax.ShapeDtypeStruct((rows, 2 * HEAD_DIM), jnp.float32),
            jax.ShapeDtypeStruct((rows, HEAD_DIM), jnp.float32),
        )
    args = (q, kv) + (() if first else state)
    return pl.pallas_call(
        functools.partial(attend_kernel, k_block, first, last),
        out_shape=out_shape,
        in_specs=[pl.BlockSpec(memory_space=pltpu.VMEM)] * len(args),
        out_specs=tuple(pl.BlockSpec(memory_space=pltpu.VMEM) for _ in out_shape),
        compiler_params=pltpu.CompilerParams(vmem_limit_bytes=24 * 2**20),
        cost_estimate=pl.CostEstimate(
            flops=8 * rows * keys * HEAD_DIM, bytes_accessed=4 * keys * HEAD_DIM, transcendentals=rows * keys
        ),
    )(*args)


def local(queries, keys, values):
    tokens = queries.shape[0]
    spare = DEVICES - HEADS * SHARE
    queries = queries.reshape(tokens, HEADS, HEAD_DIM)
    keys = keys.reshape(tokens, HEADS, HEAD_DIM)
    values = values.reshape(tokens, HEADS, HEAD_DIM)
    q = jnp.pad(queries, ((0, SHARE * Q_ROWS - tokens), (0, 0), (0, 0)))
    q = q.reshape(SHARE, 2, Q_ROWS // 2, HEADS, HEAD_DIM).transpose(3, 0, 2, 1, 4)
    q = q.reshape(HEADS * SHARE, Q_ROWS // 2, 2 * HEAD_DIM)
    kv = jnp.concatenate([keys, values], axis=-1)
    kv = kv.reshape(2, KV_ROWS, HEADS, 2 * HEAD_DIM).transpose(2, 0, 1, 3)
    kv = jnp.broadcast_to(kv[:, None], (HEADS, SHARE // 2, 2, KV_ROWS, 2 * HEAD_DIM))
    kv = kv.reshape(HEADS * SHARE, KV_ROWS, 2 * HEAD_DIM)
    sent = jnp.concatenate([jnp.pad(q, ((0, 0), (0, 1), (0, 0))), kv], axis=1)
    sent = jnp.pad(sent, ((0, spare), (0, 0), (0, 0)))
    got = lax.all_to_all(sent, AXES, 0, 0, tiled=True)
    q = got[:, : Q_ROWS // 2].reshape(DEVICES * Q_ROWS // 2, 2 * HEAD_DIM)
    kv = got[:, 8:].reshape(DEVICES * KV_ROWS, 2 * HEAD_DIM)
    other = lax.ppermute(kv, "c", [(0, 1), (1, 0)])
    state = attend(q, kv, None, False)
    (out,) = attend(q, other, state, True)
    out = out.reshape(DEVICES, Q_ROWS // 2, 2 * HEAD_DIM)
    back = lax.all_to_all(out, AXES, 0, 0, tiled=True)[: HEADS * SHARE]
    back = back.reshape(HEADS, SHARE, Q_ROWS // 2, 2, HEAD_DIM).transpose(1, 3, 2, 0, 4)
    return back.reshape(SHARE * Q_ROWS, HEADS * HEAD_DIM)[:tokens]


def solution(mesh):
    fine = Mesh(mesh.devices.reshape(SIZES), AXES)
    return jax.shard_map(
        local, mesh=fine, in_specs=(P(AXES, None),) * 3, out_specs=P(AXES, None), check_vma=False
    )
```

```python
import functools

import jax
import jax.numpy as jnp
from jax import lax
from jax.experimental import pallas as pl
from jax.experimental.pallas import tpu as pltpu
from jax.sharding import Mesh, PartitionSpec as P

HEADS = 20
HEAD_DIM = 128
PAIR = 2 * HEAD_DIM
SCALE = HEAD_DIM**-0.5 * 1.4426950408889634
AXES = ("x", "zl", "y", "zh", "c")
SIZES = (4, 2, 4, 2, 2)
COLUMNS = 16
TOKENS = 80
EXTRA = HEADS - COLUMNS
K_BLOCK = 256
STEPS = (1, 3, 2)
NT = (((1,), (1,)), ((), ()))
KV_ROWS, Q_ROWS = TOKENS, TOKENS // 2
VMEM = pl.BlockSpec(memory_space=pltpu.VMEM)
HBM = pl.BlockSpec(memory_space=pltpu.HBM)


def along_z(a, step):
    pairs = []
    for zl in range(2):
        for zh in range(2):
            z = (2 * zh + zl + step) % 4
            pairs.append((2 * zl + zh, 2 * (z % 2) + z // 2))
    return lax.ppermute(a, ("zl", "zh"), pairs)


def along(axis, a, step):
    return lax.ppermute(a, axis, [(i, (i + step) % 4) for i in range(4)])


def other_core(a):
    return lax.ppermute(a, "c", [(0, 1), (1, 0)])


def scaled_halves(q):
    full = q.astype(jnp.float32) * SCALE
    high = full.astype(jnp.bfloat16)
    low = (full - high.astype(jnp.float32)).astype(jnp.bfloat16)
    return jnp.concatenate([high, low], axis=1)


def attend_kernel(n_kv, n_after, first, last, *refs):
    refs = list(refs)
    q_ref, kv_refs, refs = refs[0], refs[1 : 1 + n_kv], refs[1 + n_kv :]
    if not first:
        acc_in, top_in = refs[:2]
        refs = refs[2:]
    refs = refs[n_after:]
    rows = q_ref.shape[0]
    ones = jnp.ones((K_BLOCK, HEAD_DIM), jnp.bfloat16)
    for half in range(2):
        lanes = slice(half * HEAD_DIM, (half + 1) * HEAD_DIM)
        here = slice(half * rows, (half + 1) * rows)
        q = scaled_halves(q_ref[:, lanes])
        if first:
            top = jnp.full((rows, 1), -1e30, jnp.float32)
            acc = jnp.zeros((rows, PAIR), jnp.float32)
        else:
            top = jnp.max(top_in[here, :], axis=1, keepdims=True)
            acc = acc_in[here, :]
        for kv_ref in kv_refs:
            for j in range(kv_ref.shape[0] // K_BLOCK):
                there = slice(j * K_BLOCK, (j + 1) * K_BLOCK)
                k = kv_ref[there, :HEAD_DIM]
                v = kv_ref[there, HEAD_DIM:]
                scores = lax.dot_general(
                    q, jnp.concatenate([k, k], axis=1), NT, preferred_element_type=jnp.float32
                )
                fresh = jnp.maximum(top, jnp.max(scores, axis=1, keepdims=True))
                weights = jnp.exp2(scores - fresh).astype(jnp.bfloat16)
                acc = acc * jnp.exp2(top - fresh) + jnp.dot(
                    weights, jnp.concatenate([v, ones], axis=1), preferred_element_type=jnp.float32
                )
                top = fresh
        if last == "out":
            refs[0][:, lanes] = (acc[:, :HEAD_DIM] / acc[:, HEAD_DIM:]).astype(jnp.bfloat16)
        elif last == "part":
            total = acc[:, HEAD_DIM:]
            part = (acc[:, :HEAD_DIM] / total).astype(jnp.bfloat16)
            level = top + jnp.log2(total)
            high = level.astype(jnp.bfloat16)
            rest = level - high.astype(jnp.float32)
            middle = rest.astype(jnp.bfloat16)
            low = (rest - middle.astype(jnp.float32)).astype(jnp.bfloat16)
            lane = lax.broadcasted_iota(jnp.int32, level.shape, 1)
            zero = jnp.zeros_like(level)
            coded = jnp.where(lane == 0, high.astype(jnp.float32), zero)
            coded = jnp.where(lane == 1, middle.astype(jnp.float32), coded)
            coded = jnp.where(lane == 2, low.astype(jnp.float32), coded)
            coded = coded.astype(jnp.bfloat16)
            for i, ref in enumerate(refs):
                some = slice(i * ref.shape[0], (i + 1) * ref.shape[0])
                ref[:, lanes] = part[some, :]
                ref[:, PAIR + half * HEAD_DIM : PAIR + (half + 1) * HEAD_DIM] = coded[some, :]
        else:
            refs[0][here, :] = acc
            refs[1][here, :] = jnp.broadcast_to(top, (rows, HEAD_DIM))


def attend(q, kvs, state, last, after=()):
    rows = q.shape[0]
    keys = sum(kv.shape[0] for kv in kvs)
    if last is None:
        out_shape = (
            jax.ShapeDtypeStruct((2 * rows, PAIR), jnp.float32),
            jax.ShapeDtypeStruct((2 * rows, HEAD_DIM), jnp.float32),
        )
    elif last == "part":
        out_shape = (jax.ShapeDtypeStruct((rows // 4, 2 * PAIR), jnp.bfloat16),) * 4
    else:
        out_shape = (jax.ShapeDtypeStruct((rows, PAIR), jnp.bfloat16),)
    args = (q, *kvs, *(state or ()))
    result = pl.pallas_call(
        functools.partial(attend_kernel, len(kvs), len(after), state is None, last),
        out_shape=out_shape,
        in_specs=[VMEM] * len(args) + [HBM] * len(after),
        out_specs=(VMEM,) * len(out_shape),
        compiler_params=pltpu.CompilerParams(vmem_limit_bytes=20 * 2**20),
        cost_estimate=pl.CostEstimate(
            flops=rows * keys * HEAD_DIM, bytes_accessed=4 * keys * HEAD_DIM, transcendentals=0
        ),
    )(*args, *after)
    return result[0] if last == "out" else result


def combine_kernel(*refs):
    parts, outs = refs[:4], refs[4:]
    for half in range(2):
        lanes = slice(half * HEAD_DIM, (half + 1) * HEAD_DIM)
        coded = slice(PAIR + half * HEAD_DIM, PAIR + (half + 1) * HEAD_DIM)
        levels = [jnp.sum(p[:, coded].astype(jnp.float32), axis=1, keepdims=True) for p in parts]
        top = functools.reduce(jnp.maximum, levels)
        shares = [jnp.exp2(level - top) for level in levels]
        total = functools.reduce(jnp.add, shares)
        summed = functools.reduce(
            jnp.add, [share * p[:, lanes].astype(jnp.float32) for share, p in zip(shares, parts, strict=True)]
        )
        whole = (summed / total).astype(jnp.bfloat16)
        for i, out in enumerate(outs):
            out[:, lanes] = whole[i * Q_ROWS : (i + 1) * Q_ROWS, :]


def combine(parts):
    rows = parts[0].shape[0]
    return pl.pallas_call(
        combine_kernel,
        out_shape=[jax.ShapeDtypeStruct((Q_ROWS, PAIR), jnp.bfloat16)] * 4,
        in_specs=[VMEM] * 4,
        out_specs=[VMEM] * 4,
        compiler_params=pltpu.CompilerParams(vmem_limit_bytes=8 * 2**20),
        cost_estimate=pl.CostEstimate(flops=16 * rows * PAIR, bytes_accessed=16 * rows * PAIR, transcendentals=0),
    )(*parts)


def fetch(sources, first, scratch, sems):
    copies = [
        pltpu.make_async_copy(source.at[:, pl.ds(first, held.shape[1])], held, sems.at[i])
        for i, (source, held) in enumerate(zip(sources, scratch, strict=True))
    ]
    for copy in copies:
        copy.start()
    for copy in copies:
        copy.wait()


def pack(out, q_ref, k_ref, v_ref, lanes):
    out[:KV_ROWS, :HEAD_DIM] = k_ref[:, lanes]
    out[:KV_ROWS, HEAD_DIM:] = v_ref[:, lanes]
    out[KV_ROWS:, :HEAD_DIM] = q_ref[:Q_ROWS, lanes]
    out[KV_ROWS:, HEAD_DIM:] = q_ref[Q_ROWS:, lanes]


def pack_extra_kernel(*refs):
    sources, outs, scratch, sems = refs[:3], refs[3:7], refs[7:10], refs[10]
    fetch(sources, COLUMNS * HEAD_DIM, scratch, sems)
    x = lax.axis_index("x")
    for step, out in zip((0, *STEPS), outs, strict=True):
        head = lax.rem(x + step, 4)
        pack(out, *scratch, pl.ds(pl.multiple_of(head * HEAD_DIM, HEAD_DIM), HEAD_DIM))


def pack_main_kernel(*refs):
    sources, out, scratch, sems = refs[:3], refs[3], refs[4:7], refs[7]
    fetch(sources, 0, scratch, sems)
    for head in range(COLUMNS):
        pack(out.at[head], *scratch, pl.ds(head * HEAD_DIM, HEAD_DIM))


def packed(kernel, arrays, shapes, columns, grant):
    return pl.pallas_call(
        kernel,
        out_shape=[jax.ShapeDtypeStruct(shape, jnp.bfloat16) for shape in shapes],
        in_specs=[HBM] * 3,
        out_specs=[VMEM] * len(shapes),
        scratch_shapes=[pltpu.VMEM((TOKENS, columns), jnp.bfloat16)] * 3 + [pltpu.SemaphoreType.DMA((3,))],
        compiler_params=pltpu.CompilerParams(vmem_limit_bytes=grant * 2**20),
        cost_estimate=pl.CostEstimate(flops=0, bytes_accessed=2**20, transcendentals=0),
    )(*arrays)


def gather_kernel(*refs):
    pieces, xkv, xq = refs[:4], refs[4], refs[5]
    for i, piece in enumerate(pieces):
        xkv[i * KV_ROWS : (i + 1) * KV_ROWS, :] = piece[:KV_ROWS, :]
        xq[i * Q_ROWS : (i + 1) * Q_ROWS, :] = piece[KV_ROWS:, :]


def gather(pieces):
    return pl.pallas_call(
        gather_kernel,
        out_shape=[jax.ShapeDtypeStruct((4 * rows, PAIR), jnp.bfloat16) for rows in (KV_ROWS, Q_ROWS)],
        in_specs=[VMEM] * 4,
        out_specs=[VMEM] * 2,
        compiler_params=pltpu.CompilerParams(vmem_limit_bytes=8 * 2**20),
        cost_estimate=pl.CostEstimate(flops=2 * 10**10, bytes_accessed=2**20, transcendentals=0),
    )(*pieces)


def sort_kernel(got, *refs):
    xkvs, xqs, (kv, both, q, xq) = refs[:4], refs[4:8], refs[8:]
    n = COLUMNS * KV_ROWS
    for i in range(COLUMNS):
        here = slice(i * KV_ROWS, (i + 1) * KV_ROWS)
        block = got[i, :KV_ROWS, :]
        kv[here, :] = block
        both[here, :] = block
        q[i * Q_ROWS : (i + 1) * Q_ROWS, :] = got[i, KV_ROWS:, :]
    for i in range(4):
        rows = xkvs[i].shape[0]
        both[n + i * rows : n + (i + 1) * rows, :] = xkvs[i][...]
        rows = xqs[i].shape[0]
        xq[i * rows : (i + 1) * rows, :] = xqs[i][...]


def sort(got, xkvs, xqs):
    kv, q = COLUMNS * KV_ROWS, COLUMNS * Q_ROWS
    return pl.pallas_call(
        sort_kernel,
        out_shape=[jax.ShapeDtypeStruct((rows, PAIR), jnp.bfloat16) for rows in (kv, 2 * kv, q, q)],
        in_specs=[VMEM] * 9,
        out_specs=[VMEM] * 4,
        compiler_params=pltpu.CompilerParams(vmem_limit_bytes=16 * 2**20),
        cost_estimate=pl.CostEstimate(flops=0, bytes_accessed=2**20, transcendentals=0),
    )(got, *xkvs, *xqs)


def beside_kernel(a, b, *refs):
    both, first, second = refs[-3:]
    rows = a.shape[0]
    both[:rows, :] = a[...]
    both[rows:, :] = b[...]
    first[...] = a[: first.shape[0], :]
    second[...] = b[first.shape[0] :, :]


def beside(a, b, *after):
    rows = (2 * a.shape[0], 3 * K_BLOCK, a.shape[0] - 3 * K_BLOCK)
    return pl.pallas_call(
        beside_kernel,
        out_shape=[jax.ShapeDtypeStruct((count, PAIR), jnp.bfloat16) for count in rows],
        in_specs=[VMEM, VMEM] + [HBM] * len(after),
        out_specs=[VMEM] * 3,
        compiler_params=pltpu.CompilerParams(vmem_limit_bytes=12 * 2**20),
        cost_estimate=pl.CostEstimate(flops=0, bytes_accessed=2**20, transcendentals=0),
    )(a, b, *after)


def join_kernel(a, b, after, out):
    out[: a.shape[0], :] = a[...]
    out[a.shape[0] :, :] = b[...]


def join(a, b, after):
    return pl.pallas_call(
        join_kernel,
        out_shape=jax.ShapeDtypeStruct((a.shape[0] + b.shape[0], PAIR), jnp.bfloat16),
        in_specs=[VMEM, VMEM, HBM],
        out_specs=VMEM,
        compiler_params=pltpu.CompilerParams(vmem_limit_bytes=8 * 2**20),
        cost_estimate=pl.CostEstimate(flops=0, bytes_accessed=2**20, transcendentals=0),
    )(a, b, after)


def unpack_kernel(main, *refs):
    extra, out = refs[:4], refs[4]

    def put(block, lanes):
        out[:Q_ROWS, lanes] = block[:, :HEAD_DIM]
        out[Q_ROWS:, lanes] = block[:, HEAD_DIM:]

    for head in range(COLUMNS):
        put(main.at[head], pl.ds(head * HEAD_DIM, HEAD_DIM))
    x = lax.axis_index("x")
    for step, block in zip((0, *STEPS), extra, strict=True):
        head = COLUMNS + lax.rem(x + step, 4)
        put(block, pl.ds(pl.multiple_of(head * HEAD_DIM, HEAD_DIM), HEAD_DIM))


def unpack(main, extra):
    return pl.pallas_call(
        unpack_kernel,
        out_shape=jax.ShapeDtypeStruct((TOKENS, HEADS * HEAD_DIM), jnp.bfloat16),
        in_specs=[VMEM] * 5,
        out_specs=VMEM,
        compiler_params=pltpu.CompilerParams(vmem_limit_bytes=8 * 2**20),
        cost_estimate=pl.CostEstimate(flops=0, bytes_accessed=2**20, transcendentals=0),
    )(main, *extra)


def local(queries, keys, values):
    arrays = (queries, keys, values)
    rows = KV_ROWS + Q_ROWS
    extra = packed(pack_extra_kernel, arrays, [(rows, PAIR)] * 4, EXTRA * HEAD_DIM, 60)
    (sent,) = packed(pack_main_kernel, arrays, [(COLUMNS, rows, PAIR)], COLUMNS * HEAD_DIM, 12)

    extra = [extra[0]] + [along("x", a, step) for a, step in zip(extra[1:], STEPS, strict=True)]
    xkv, xq = gather(extra)
    xqs = [xq] + [along("y", xq, step) for step in STEPS]
    xkvs = [xkv] + [along_z(xkv, step) for step in STEPS]

    got = lax.all_to_all(sent, ("x", "y"), 0, 0, tiled=True)
    kv, both, q, xq = sort(got, xkvs, xqs)
    kv_next, kv_before = along_z(kv, 1), along_z(kv, 3)
    other = other_core(both)

    rows = kv.shape[0]
    parts = attend(xq, [both[rows:], other[rows:]], None, "part")
    back = [along("y", part, -step) for part, step in zip(parts[1:], STEPS, strict=True)]
    state = attend(q, [kv, other[:rows]], None, None)
    xout = combine([parts[0], *back])

    near, first, second = beside(kv_next, kv_before, state[0], *back)
    first, second = along_z(first, 1), along_z(second, 3)
    state = attend(q, [near, other_core(near)], state, None)
    across = join(first, second, state[0])
    out = attend(q, [across, other_core(across)], state, "out", xout[:1])
    out = lax.all_to_all(out.reshape(COLUMNS, Q_ROWS, PAIR), ("x", "y"), 0, 0, tiled=True)
    xout = [xout[0]] + [along("x", a, -step) for a, step in zip(xout[1:], STEPS, strict=True)]
    return unpack(out, xout)


def solution(mesh):
    fine = Mesh(mesh.devices.reshape(SIZES), AXES)
    return jax.shard_map(
        local, mesh=fine, in_specs=(P(AXES, None),) * 3, out_specs=P(AXES, None), check_vma=False
    )
```

```python
import functools

import jax
import jax.numpy as jnp
from jax import lax
from jax.experimental import pallas as pl
from jax.experimental.pallas import tpu as pltpu
from jax.sharding import Mesh, PartitionSpec as P

HEADS = 20
HEAD_DIM = 128
PAIR = 2 * HEAD_DIM
SCALE = HEAD_DIM**-0.5 * 1.4426950408889634
AXES = ("x", "zl", "y", "zh", "c")
SIZES = (4, 2, 4, 2, 2)
COLUMNS = 16
TOKENS = 80
EXTRA = HEADS - COLUMNS
K_BLOCK = 256
STEPS = (1, 3, 2)
NT = (((1,), (1,)), ((), ()))
KV_ROWS, Q_ROWS = TOKENS, TOKENS // 2
VMEM = pl.BlockSpec(memory_space=pltpu.VMEM)
HBM = pl.BlockSpec(memory_space=pltpu.HBM)


def along_z(a, step):
    pairs = []
    for zl in range(2):
        for zh in range(2):
            z = (2 * zh + zl + step) % 4
            pairs.append((2 * zl + zh, 2 * (z % 2) + z // 2))
    return lax.ppermute(a, ("zl", "zh"), pairs)


def along(axis, a, step):
    return lax.ppermute(a, axis, [(i, (i + step) % 4) for i in range(4)])


def other_core(a):
    return lax.ppermute(a, "c", [(0, 1), (1, 0)])


def scaled_halves(q):
    full = q.astype(jnp.float32) * SCALE
    high = full.astype(jnp.bfloat16)
    low = (full - high.astype(jnp.float32)).astype(jnp.bfloat16)
    return jnp.concatenate([high, low], axis=1)


def attend_kernel(n_kv, n_after, first, last, *refs):
    refs = list(refs)
    q_ref, kv_refs, refs = refs[0], refs[1 : 1 + n_kv], refs[1 + n_kv :]
    if not first:
        acc_in, top_in = refs[:2]
        refs = refs[2:]
    refs = refs[n_after:]
    rows = q_ref.shape[0]
    ones = jnp.ones((K_BLOCK, HEAD_DIM), jnp.bfloat16)
    for half in range(2):
        lanes = slice(half * HEAD_DIM, (half + 1) * HEAD_DIM)
        here = slice(half * rows, (half + 1) * rows)
        q = scaled_halves(q_ref[:, lanes])
        if first:
            top = jnp.full((rows, 1), -1e30, jnp.float32)
            acc = jnp.zeros((rows, PAIR), jnp.float32)
        else:
            top = jnp.max(top_in[here, :], axis=1, keepdims=True)
            acc = acc_in[here, :]
        for kv_ref in kv_refs:
            for j in range(kv_ref.shape[0] // K_BLOCK):
                there = slice(j * K_BLOCK, (j + 1) * K_BLOCK)
                k = kv_ref[there, :HEAD_DIM]
                v = kv_ref[there, HEAD_DIM:]
                scores = lax.dot_general(
                    q, jnp.concatenate([k, k], axis=1), NT, preferred_element_type=jnp.float32
                )
                fresh = jnp.maximum(top, jnp.max(scores, axis=1, keepdims=True))
                weights = jnp.exp2(scores - fresh).astype(jnp.bfloat16)
                acc = acc * jnp.exp2(top - fresh) + jnp.dot(
                    weights, jnp.concatenate([v, ones], axis=1), preferred_element_type=jnp.float32
                )
                top = fresh
        if last == "out":
            refs[0][:, lanes] = (acc[:, :HEAD_DIM] / acc[:, HEAD_DIM:]).astype(jnp.bfloat16)
        elif last == "part":
            total = acc[:, HEAD_DIM:]
            part = (acc[:, :HEAD_DIM] / total).astype(jnp.bfloat16)
            level = top + jnp.log2(total)
            high = level.astype(jnp.bfloat16)
            rest = level - high.astype(jnp.float32)
            middle = rest.astype(jnp.bfloat16)
            low = (rest - middle.astype(jnp.float32)).astype(jnp.bfloat16)
            lane = lax.broadcasted_iota(jnp.int32, level.shape, 1)
            zero = jnp.zeros_like(level)
            coded = jnp.where(lane == 0, high.astype(jnp.float32), zero)
            coded = jnp.where(lane == 1, middle.astype(jnp.float32), coded)
            coded = jnp.where(lane == 2, low.astype(jnp.float32), coded)
            coded = coded.astype(jnp.bfloat16)
            for i, ref in enumerate(refs):
                some = slice(i * ref.shape[0], (i + 1) * ref.shape[0])
                ref[:, lanes] = part[some, :]
                ref[:, PAIR + half * HEAD_DIM : PAIR + (half + 1) * HEAD_DIM] = coded[some, :]
        else:
            refs[0][here, :] = acc
            refs[1][here, :] = jnp.broadcast_to(top, (rows, HEAD_DIM))


def attend(q, kvs, state, last, after=()):
    rows = q.shape[0]
    keys = sum(kv.shape[0] for kv in kvs)
    if last is None:
        out_shape = (
            jax.ShapeDtypeStruct((2 * rows, PAIR), jnp.float32),
            jax.ShapeDtypeStruct((2 * rows, HEAD_DIM), jnp.float32),
        )
    elif last == "part":
        out_shape = (jax.ShapeDtypeStruct((rows // 4, 2 * PAIR), jnp.bfloat16),) * 4
    else:
        out_shape = (jax.ShapeDtypeStruct((rows, PAIR), jnp.bfloat16),)
    args = (q, *kvs, *(state or ()))
    result = pl.pallas_call(
        functools.partial(attend_kernel, len(kvs), len(after), state is None, last),
        out_shape=out_shape,
        in_specs=[VMEM] * len(args) + [HBM] * len(after),
        out_specs=(VMEM,) * len(out_shape),
        compiler_params=pltpu.CompilerParams(vmem_limit_bytes=20 * 2**20),
        cost_estimate=pl.CostEstimate(
            flops=rows * keys * HEAD_DIM, bytes_accessed=4 * keys * HEAD_DIM, transcendentals=0
        ),
    )(*args, *after)
    return result[0] if last == "out" else result


def combine_kernel(*refs):
    parts, outs = refs[:4], refs[4:]
    for half in range(2):
        lanes = slice(half * HEAD_DIM, (half + 1) * HEAD_DIM)
        coded = slice(PAIR + half * HEAD_DIM, PAIR + (half + 1) * HEAD_DIM)
        levels = [jnp.sum(p[:, coded].astype(jnp.float32), axis=1, keepdims=True) for p in parts]
        top = functools.reduce(jnp.maximum, levels)
        shares = [jnp.exp2(level - top) for level in levels]
        total = functools.reduce(jnp.add, shares)
        summed = functools.reduce(
            jnp.add, [share * p[:, lanes].astype(jnp.float32) for share, p in zip(shares, parts, strict=True)]
        )
        whole = (summed / total).astype(jnp.bfloat16)
        for i, out in enumerate(outs):
            out[:, lanes] = whole[i * Q_ROWS : (i + 1) * Q_ROWS, :]


def combine(parts):
    rows = parts[0].shape[0]
    return pl.pallas_call(
        combine_kernel,
        out_shape=[jax.ShapeDtypeStruct((Q_ROWS, PAIR), jnp.bfloat16)] * 4,
        in_specs=[VMEM] * 4,
        out_specs=[VMEM] * 4,
        compiler_params=pltpu.CompilerParams(vmem_limit_bytes=8 * 2**20),
        cost_estimate=pl.CostEstimate(flops=16 * rows * PAIR, bytes_accessed=16 * rows * PAIR, transcendentals=0),
    )(*parts)


def fetch(sources, first, scratch, sems):
    copies = [
        pltpu.make_async_copy(source.at[:, pl.ds(first, held.shape[1])], held, sems.at[i])
        for i, (source, held) in enumerate(zip(sources, scratch, strict=True))
    ]
    for copy in copies:
        copy.start()
    for copy in copies:
        copy.wait()


def pack(out, q_ref, k_ref, v_ref, lanes):
    out[:KV_ROWS, :HEAD_DIM] = k_ref[:, lanes]
    out[:KV_ROWS, HEAD_DIM:] = v_ref[:, lanes]
    out[KV_ROWS:, :HEAD_DIM] = q_ref[:Q_ROWS, lanes]
    out[KV_ROWS:, HEAD_DIM:] = q_ref[Q_ROWS:, lanes]


def pack_extra_kernel(*refs):
    sources, outs, scratch, sems = refs[:3], refs[3:7], refs[7:10], refs[10]
    fetch(sources, COLUMNS * HEAD_DIM, scratch, sems)
    x = lax.axis_index("x")
    for step, out in zip((0, *STEPS), outs, strict=True):
        head = lax.rem(x + step, 4)
        pack(out, *scratch, pl.ds(pl.multiple_of(head * HEAD_DIM, HEAD_DIM), HEAD_DIM))


def pack_main_kernel(*refs):
    sources, out, scratch, sems = refs[:3], refs[3], refs[4:7], refs[7]
    fetch(sources, 0, scratch, sems)
    for head in range(COLUMNS):
        pack(out.at[head], *scratch, pl.ds(head * HEAD_DIM, HEAD_DIM))


def packed(kernel, arrays, shapes, columns, grant):
    return pl.pallas_call(
        kernel,
        out_shape=[jax.ShapeDtypeStruct(shape, jnp.bfloat16) for shape in shapes],
        in_specs=[HBM] * 3,
        out_specs=[VMEM] * len(shapes),
        scratch_shapes=[pltpu.VMEM((TOKENS, columns), jnp.bfloat16)] * 3 + [pltpu.SemaphoreType.DMA((3,))],
        compiler_params=pltpu.CompilerParams(vmem_limit_bytes=grant * 2**20),
        cost_estimate=pl.CostEstimate(flops=0, bytes_accessed=2**20, transcendentals=0),
    )(*arrays)


def gather_kernel(*refs):
    pieces, xkv, xq = refs[:4], refs[4], refs[5]
    for i, piece in enumerate(pieces):
        xkv[i * KV_ROWS : (i + 1) * KV_ROWS, :] = piece[:KV_ROWS, :]
        xq[i * Q_ROWS : (i + 1) * Q_ROWS, :] = piece[KV_ROWS:, :]


def gather(pieces):
    return pl.pallas_call(
        gather_kernel,
        out_shape=[jax.ShapeDtypeStruct((4 * rows, PAIR), jnp.bfloat16) for rows in (KV_ROWS, Q_ROWS)],
        in_specs=[VMEM] * 4,
        out_specs=[VMEM] * 2,
        compiler_params=pltpu.CompilerParams(vmem_limit_bytes=8 * 2**20),
        cost_estimate=pl.CostEstimate(flops=2 * 10**10, bytes_accessed=2**20, transcendentals=0),
    )(*pieces)


def sort_kernel(got, kv, q):
    for i in range(COLUMNS):
        kv[i * KV_ROWS : (i + 1) * KV_ROWS, :] = got[i, :KV_ROWS, :]
        q[i * Q_ROWS : (i + 1) * Q_ROWS, :] = got[i, KV_ROWS:, :]


def sort(got):
    return pl.pallas_call(
        sort_kernel,
        out_shape=[jax.ShapeDtypeStruct((COLUMNS * rows, PAIR), jnp.bfloat16) for rows in (KV_ROWS, Q_ROWS)],
        in_specs=[VMEM],
        out_specs=[VMEM] * 2,
        compiler_params=pltpu.CompilerParams(vmem_limit_bytes=12 * 2**20),
        cost_estimate=pl.CostEstimate(flops=0, bytes_accessed=2**20, transcendentals=0),
    )(got)


def stack_kernel(*refs):
    out, start = refs[-1], 0
    for ref in refs[:-1]:
        out[start : start + ref.shape[0], :] = ref[...]
        start += ref.shape[0]


def stack(*pieces, flops=0):
    return pl.pallas_call(
        stack_kernel,
        out_shape=jax.ShapeDtypeStruct((sum(piece.shape[0] for piece in pieces), PAIR), jnp.bfloat16),
        in_specs=[VMEM] * len(pieces),
        out_specs=VMEM,
        compiler_params=pltpu.CompilerParams(vmem_limit_bytes=12 * 2**20),
        cost_estimate=pl.CostEstimate(flops=flops, bytes_accessed=2**20, transcendentals=0),
    )(*pieces)


def beside_kernel(a, b, *refs):
    both, first, second = refs[-3:]
    rows = a.shape[0]
    both[:rows, :] = a[...]
    both[rows:, :] = b[...]
    first[...] = a[: first.shape[0], :]
    second[...] = b[first.shape[0] :, :]


def beside(a, b, *after):
    rows = (2 * a.shape[0], a.shape[0] // 2, a.shape[0] // 2)
    return pl.pallas_call(
        beside_kernel,
        out_shape=[jax.ShapeDtypeStruct((count, PAIR), jnp.bfloat16) for count in rows],
        in_specs=[VMEM, VMEM] + [HBM] * len(after),
        out_specs=[VMEM] * 3,
        compiler_params=pltpu.CompilerParams(vmem_limit_bytes=12 * 2**20),
        cost_estimate=pl.CostEstimate(flops=0, bytes_accessed=2**20, transcendentals=0),
    )(a, b, *after)


def join_kernel(a, b, after, out):
    out[: a.shape[0], :] = a[...]
    out[a.shape[0] :, :] = b[...]


def join(a, b, after):
    return pl.pallas_call(
        join_kernel,
        out_shape=jax.ShapeDtypeStruct((a.shape[0] + b.shape[0], PAIR), jnp.bfloat16),
        in_specs=[VMEM, VMEM, HBM],
        out_specs=VMEM,
        compiler_params=pltpu.CompilerParams(vmem_limit_bytes=8 * 2**20),
        cost_estimate=pl.CostEstimate(flops=0, bytes_accessed=2**20, transcendentals=0),
    )(a, b, after)


def unpack_kernel(main, *refs):
    extra, out = refs[:4], refs[4]

    def put(block, lanes):
        out[:Q_ROWS, lanes] = block[:, :HEAD_DIM]
        out[Q_ROWS:, lanes] = block[:, HEAD_DIM:]

    for head in range(COLUMNS):
        put(main.at[head], pl.ds(head * HEAD_DIM, HEAD_DIM))
    x = lax.axis_index("x")
    for step, block in zip((0, *STEPS), extra, strict=True):
        head = COLUMNS + lax.rem(x + step, 4)
        put(block, pl.ds(pl.multiple_of(head * HEAD_DIM, HEAD_DIM), HEAD_DIM))


def unpack(main, extra):
    return pl.pallas_call(
        unpack_kernel,
        out_shape=jax.ShapeDtypeStruct((TOKENS, HEADS * HEAD_DIM), jnp.bfloat16),
        in_specs=[VMEM] * 5,
        out_specs=VMEM,
        compiler_params=pltpu.CompilerParams(vmem_limit_bytes=8 * 2**20),
        cost_estimate=pl.CostEstimate(flops=0, bytes_accessed=2**20, transcendentals=0),
    )(main, *extra)


def local(queries, keys, values):
    arrays = (queries, keys, values)
    rows = KV_ROWS + Q_ROWS
    extra = packed(pack_extra_kernel, arrays, [(rows, PAIR)] * 4, EXTRA * HEAD_DIM, 60)
    (sent,) = packed(pack_main_kernel, arrays, [(COLUMNS, rows, PAIR)], COLUMNS * HEAD_DIM, 12)

    extra = [extra[0]] + [along("x", a, step) for a, step in zip(extra[1:], STEPS, strict=True)]
    xkv, xq = gather(extra)
    xqs = [xq] + [along("y", xq, step) for step in STEPS]
    xkvs = [xkv, along_z(xkv, 1), along_z(xkv, 3)]
    xkvs.append(along_z(xkvs[1], 1))

    got = lax.all_to_all(sent, ("x", "y"), 0, 0, tiled=True)
    kv, q = sort(got)
    kv_next, kv_before = along_z(kv, 1), along_z(kv, 3)
    both, xq = stack(kv, *xkvs), stack(*xqs, flops=2 * 10**10)
    other = other_core(both)

    rows = kv.shape[0]
    parts = attend(xq, [both[rows:], other[rows:]], None, "part")
    back = [along("y", part, -step) for part, step in zip(parts[1:], STEPS, strict=True)]
    state = attend(q, [kv, other[:rows]], None, None)
    xout = combine([parts[0], *back])

    near, first, second = beside(kv_next, kv_before, state[0], *back)
    first, second = along_z(first, 1), along_z(second, 3)
    state = attend(q, [near, other_core(near)], state, None)
    across = join(first, second, state[0])
    out = attend(q, [across, other_core(across)], state, "out", xout[:1])
    out = lax.all_to_all(out.reshape(COLUMNS, Q_ROWS, PAIR), ("x", "y"), 0, 0, tiled=True)
    xout = [xout[0]] + [along("x", a, -step) for a, step in zip(xout[1:], STEPS, strict=True)]
    return unpack(out, xout)


def solution(mesh):
    fine = Mesh(mesh.devices.reshape(SIZES), AXES)
    return jax.shard_map(
        local, mesh=fine, in_specs=(P(AXES, None),) * 3, out_specs=P(AXES, None), check_vma=False
    )
```

```python
import functools

import jax
import jax.numpy as jnp
from jax import lax
from jax.experimental import pallas as pl
from jax.experimental.pallas import tpu as pltpu
from jax.sharding import Mesh, PartitionSpec as P

HEADS = 20
HEAD_DIM = 128
PAIR = 2 * HEAD_DIM
SCALE = HEAD_DIM**-0.5 * 1.4426950408889634
AXES = ("x", "zl", "y", "zh", "c")
SIZES = (4, 2, 4, 2, 2)
COLUMNS = 16
TOKENS = 80
EXTRA = HEADS - COLUMNS
K_BLOCK = 256
CODE_ROWS = 16
STEPS = (1, 3, 2)
NT = (((1,), (1,)), ((), ()))
KV_ROWS, Q_ROWS = TOKENS, TOKENS // 2
VMEM = pl.BlockSpec(memory_space=pltpu.VMEM)
HBM = pl.BlockSpec(memory_space=pltpu.HBM)


def along_z(a, step):
    pairs = []
    for zl in range(2):
        for zh in range(2):
            z = (2 * zh + zl + step) % 4
            pairs.append((2 * zl + zh, 2 * (z % 2) + z // 2))
    return lax.ppermute(a, ("zl", "zh"), pairs)


def along(axis, a, step):
    return lax.ppermute(a, axis, [(i, (i + step) % 4) for i in range(4)])


def key_partner(a):
    return lax.ppermute(a, "zl", [(0, 1), (1, 0)])


def query_partner(a):
    return lax.ppermute(a, ("zl", "zh"), [(0, 3), (3, 0), (1, 2), (2, 1)])


def other_core(a):
    return lax.ppermute(a, "c", [(0, 1), (1, 0)])


def scaled_halves(q):
    full = q.astype(jnp.float32) * SCALE
    high = full.astype(jnp.bfloat16)
    low = (full - high.astype(jnp.float32)).astype(jnp.bfloat16)
    return jnp.concatenate([high, low], axis=1)


def diagonal():
    shape = (HEAD_DIM, HEAD_DIM)
    return lax.broadcasted_iota(jnp.int32, shape, 0) == lax.broadcasted_iota(jnp.int32, shape, 1)


def coded_rows(level):
    blocks = level.shape[0] // HEAD_DIM
    row = lax.broadcasted_iota(jnp.int32, (CODE_ROWS, HEAD_DIM), 0)
    coded = jnp.zeros((CODE_ROWS, HEAD_DIM), jnp.float32)
    for i in range(blocks):
        block = jnp.where(diagonal(), level[i * HEAD_DIM : (i + 1) * HEAD_DIM, :], 0.0)
        rest = jnp.sum(block, axis=0, keepdims=True)
        for term in range(3):
            rounded = rest.astype(jnp.bfloat16).astype(jnp.float32)
            coded = jnp.where(row == term * blocks + i, rounded, coded)
            rest = rest - rounded
    return coded


def decoded_column(coded, i, blocks):
    row = lax.broadcasted_iota(jnp.int32, coded.shape, 0)
    mine = (row == i) | (row == blocks + i) | (row == 2 * blocks + i)
    numbers = jnp.sum(jnp.where(mine, coded, 0.0), axis=0, keepdims=True)
    return jnp.sum(jnp.where(diagonal(), numbers, 0.0), axis=1, keepdims=True)


def attend_kernel(n_kv, n_after, first, last, *refs):
    refs = list(refs)
    q_ref, kv_refs, refs = refs[0], refs[1 : 1 + n_kv], refs[1 + n_kv :]
    if not first:
        acc_in, top_in = refs[:2]
        refs = refs[2:]
    refs = refs[n_after:]
    rows = q_ref.shape[0]
    ones = jnp.ones((K_BLOCK, HEAD_DIM), jnp.bfloat16)
    for half in range(2):
        lanes = slice(half * HEAD_DIM, (half + 1) * HEAD_DIM)
        here = slice(half * rows, (half + 1) * rows)
        q = scaled_halves(q_ref[:, lanes])
        if first:
            top = jnp.full((rows, 1), -1e30, jnp.float32)
            acc = jnp.zeros((rows, PAIR), jnp.float32)
        else:
            top = jnp.max(top_in[here, :], axis=1, keepdims=True)
            acc = acc_in[here, :]
        for kv_ref in kv_refs:
            for j in range(kv_ref.shape[0] // K_BLOCK):
                there = slice(j * K_BLOCK, (j + 1) * K_BLOCK)
                k = kv_ref[there, :HEAD_DIM]
                v = kv_ref[there, HEAD_DIM:]
                scores = lax.dot_general(
                    q, jnp.concatenate([k, k], axis=1), NT, preferred_element_type=jnp.float32
                )
                fresh = jnp.maximum(top, jnp.max(scores, axis=1, keepdims=True))
                weights = jnp.exp2(scores - fresh).astype(jnp.bfloat16)
                acc = acc * jnp.exp2(top - fresh) + jnp.dot(
                    weights, jnp.concatenate([v, ones], axis=1), preferred_element_type=jnp.float32
                )
                top = fresh
        if last == "send":
            total = acc[:, HEAD_DIM:]
            refs[0][:rows, lanes] = (acc[:, :HEAD_DIM] / total).astype(jnp.bfloat16)
            refs[0][rows:, lanes] = coded_rows(top + jnp.log2(total)).astype(jnp.bfloat16)
        elif last == "part":
            total = acc[:, HEAD_DIM:]
            part = (acc[:, :HEAD_DIM] / total).astype(jnp.bfloat16)
            coded = coded_rows(top + jnp.log2(total)).astype(jnp.bfloat16)
            some = rows // 4
            for i, ref in enumerate(refs):
                ref[:some, lanes] = part[i * some : (i + 1) * some, :]
                ref[some:, lanes] = coded
        else:
            refs[0][here, :] = acc
            refs[1][here, :] = jnp.broadcast_to(top, (rows, HEAD_DIM))


def attend(q, kvs, state, last, after=(), flops=0):
    rows = q.shape[0]
    keys = sum(kv.shape[0] for kv in kvs)
    if last is None:
        out_shape = (
            jax.ShapeDtypeStruct((2 * rows, PAIR), jnp.float32),
            jax.ShapeDtypeStruct((2 * rows, HEAD_DIM), jnp.float32),
        )
    elif last == "part":
        out_shape = (jax.ShapeDtypeStruct((rows // 4 + CODE_ROWS, PAIR), jnp.bfloat16),) * 4
    else:
        out_shape = (jax.ShapeDtypeStruct((rows + CODE_ROWS, PAIR), jnp.bfloat16),)
    args = (q, *kvs, *(state or ()))
    result = pl.pallas_call(
        functools.partial(attend_kernel, len(kvs), len(after), state is None, last),
        out_shape=out_shape,
        in_specs=[VMEM] * len(args) + [HBM] * len(after),
        out_specs=(VMEM,) * len(out_shape),
        compiler_params=pltpu.CompilerParams(vmem_limit_bytes=20 * 2**20),
        cost_estimate=pl.CostEstimate(
            flops=flops, bytes_accessed=4 * keys * HEAD_DIM, transcendentals=0
        ),
    )(*args, *after)
    return result[0] if last == "send" else result


def combine_kernel(*refs):
    parts, outs = refs[:4], refs[4:]
    rows = parts[0].shape[0] - CODE_ROWS
    blocks = 4 * rows // HEAD_DIM
    for half in range(2):
        lanes = slice(half * HEAD_DIM, (half + 1) * HEAD_DIM)
        levels = []
        for i, part in enumerate(parts):
            first, start = divmod(i * rows, HEAD_DIM)
            coded = part[rows:, lanes].astype(jnp.float32)
            column = jnp.concatenate([decoded_column(coded, first + j, blocks) for j in range(2)], axis=0)
            levels.append(column[start : start + rows, :])
        top = functools.reduce(jnp.maximum, levels)
        shares = [jnp.exp2(level - top) for level in levels]
        total = functools.reduce(jnp.add, shares)
        summed = functools.reduce(
            jnp.add, [share * p[:rows, lanes].astype(jnp.float32) for share, p in zip(shares, parts, strict=True)]
        )
        whole = (summed / total).astype(jnp.bfloat16)
        for i, out in enumerate(outs):
            out[:, lanes] = whole[i * Q_ROWS : (i + 1) * Q_ROWS, :]


def combine(parts):
    rows = parts[0].shape[0]
    return pl.pallas_call(
        combine_kernel,
        out_shape=[jax.ShapeDtypeStruct((Q_ROWS, PAIR), jnp.bfloat16)] * 4,
        in_specs=[VMEM] * 4,
        out_specs=[VMEM] * 4,
        compiler_params=pltpu.CompilerParams(vmem_limit_bytes=8 * 2**20),
        cost_estimate=pl.CostEstimate(flops=16 * rows * PAIR, bytes_accessed=16 * rows * PAIR, transcendentals=0),
    )(*parts)


def fetch(sources, first, scratch, sems):
    copies = [
        pltpu.make_async_copy(source.at[:, pl.ds(first, held.shape[1])], held, sems.at[i])
        for i, (source, held) in enumerate(zip(sources, scratch, strict=True))
    ]
    for copy in copies:
        copy.start()
    for copy in copies:
        copy.wait()


def pack(out, q_ref, k_ref, v_ref, lanes):
    out[:KV_ROWS, :HEAD_DIM] = k_ref[:, lanes]
    out[:KV_ROWS, HEAD_DIM:] = v_ref[:, lanes]
    out[KV_ROWS:, :HEAD_DIM] = q_ref[:Q_ROWS, lanes]
    out[KV_ROWS:, HEAD_DIM:] = q_ref[Q_ROWS:, lanes]


def pack_extra_kernel(*refs):
    sources, outs, scratch, sems = refs[:3], refs[3:7], refs[7:10], refs[10]
    fetch(sources, COLUMNS * HEAD_DIM, scratch, sems)
    x = lax.axis_index("x")
    for step, out in zip((0, *STEPS), outs, strict=True):
        head = lax.rem(x + step, 4)
        pack(out, *scratch, pl.ds(pl.multiple_of(head * HEAD_DIM, HEAD_DIM), HEAD_DIM))


def pack_main_kernel(*refs):
    sources, out, scratch, sems = refs[:3], refs[3], refs[4:7], refs[7]
    fetch(sources, 0, scratch, sems)
    for head in range(COLUMNS):
        pack(out.at[head], *scratch, pl.ds(head * HEAD_DIM, HEAD_DIM))


def packed(kernel, arrays, shapes, columns, grant):
    return pl.pallas_call(
        kernel,
        out_shape=[jax.ShapeDtypeStruct(shape, jnp.bfloat16) for shape in shapes],
        in_specs=[HBM] * 3,
        out_specs=[VMEM] * len(shapes),
        scratch_shapes=[pltpu.VMEM((TOKENS, columns), jnp.bfloat16)] * 3 + [pltpu.SemaphoreType.DMA((3,))],
        compiler_params=pltpu.CompilerParams(vmem_limit_bytes=grant * 2**20),
        cost_estimate=pl.CostEstimate(flops=0, bytes_accessed=2**20, transcendentals=0),
    )(*arrays)


def gather_kernel(*refs):
    pieces, xkv, xq = refs[:4], refs[4], refs[5]
    for i, piece in enumerate(pieces):
        xkv[i * KV_ROWS : (i + 1) * KV_ROWS, :] = piece[:KV_ROWS, :]
        xq[i * Q_ROWS : (i + 1) * Q_ROWS, :] = piece[KV_ROWS:, :]


def gather(pieces):
    return pl.pallas_call(
        gather_kernel,
        out_shape=[jax.ShapeDtypeStruct((4 * rows, PAIR), jnp.bfloat16) for rows in (KV_ROWS, Q_ROWS)],
        in_specs=[VMEM] * 4,
        out_specs=[VMEM] * 2,
        compiler_params=pltpu.CompilerParams(vmem_limit_bytes=8 * 2**20),
        cost_estimate=pl.CostEstimate(flops=2 * 10**10, bytes_accessed=2**20, transcendentals=0),
    )(*pieces)


def sort_kernel(got, kv, q):
    for i in range(COLUMNS):
        kv[i * KV_ROWS : (i + 1) * KV_ROWS, :] = got[i, :KV_ROWS, :]
        q[i * Q_ROWS : (i + 1) * Q_ROWS, :] = got[i, KV_ROWS:, :]


def sort(got):
    return pl.pallas_call(
        sort_kernel,
        out_shape=[jax.ShapeDtypeStruct((COLUMNS * rows, PAIR), jnp.bfloat16) for rows in (KV_ROWS, Q_ROWS)],
        in_specs=[VMEM],
        out_specs=[VMEM] * 2,
        compiler_params=pltpu.CompilerParams(vmem_limit_bytes=12 * 2**20),
        cost_estimate=pl.CostEstimate(flops=0, bytes_accessed=2**20, transcendentals=0),
    )(got)


def stack_kernel(*refs):
    out, start = refs[-1], 0
    for ref in refs[:-1]:
        out[start : start + ref.shape[0], :] = ref[...]
        start += ref.shape[0]


def stack(*pieces, flops=0):
    return pl.pallas_call(
        stack_kernel,
        out_shape=jax.ShapeDtypeStruct((sum(piece.shape[0] for piece in pieces), PAIR), jnp.bfloat16),
        in_specs=[VMEM] * len(pieces),
        out_specs=VMEM,
        compiler_params=pltpu.CompilerParams(vmem_limit_bytes=12 * 2**20),
        cost_estimate=pl.CostEstimate(flops=flops, bytes_accessed=2**20, transcendentals=0),
    )(*pieces)


def hold_kernel(a, *refs):
    refs[-1][...] = a[...]


def hold(a, *after):
    return pl.pallas_call(
        hold_kernel,
        out_shape=jax.ShapeDtypeStruct(a.shape, a.dtype),
        in_specs=[VMEM] + [HBM] * len(after),
        out_specs=VMEM,
        compiler_params=pltpu.CompilerParams(vmem_limit_bytes=12 * 2**20),
        cost_estimate=pl.CostEstimate(flops=0, bytes_accessed=2**20, transcendentals=0),
    )(a, *after)


def merge_kernel(acc, top, sent, out):
    rows = out.shape[0]
    blocks = rows // HEAD_DIM
    for half in range(2):
        lanes = slice(half * HEAD_DIM, (half + 1) * HEAD_DIM)
        coded = sent[rows:, lanes].astype(jnp.float32)
        for i in range(blocks):
            there = slice(i * HEAD_DIM, (i + 1) * HEAD_DIM)
            here = slice(half * rows + i * HEAD_DIM, half * rows + (i + 1) * HEAD_DIM)
            total = acc[here, HEAD_DIM:]
            level = top[here, :] + jnp.log2(total)
            other = decoded_column(coded, i, blocks)
            largest = jnp.maximum(level, other)
            share, other = jnp.exp2(level - largest), jnp.exp2(other - largest)
            summed = acc[here, :HEAD_DIM] / total * share + sent[there, lanes].astype(jnp.float32) * other
            out[there, lanes] = (summed / (share + other)).astype(jnp.bfloat16)


def merge(acc, top, sent):
    return pl.pallas_call(
        merge_kernel,
        out_shape=jax.ShapeDtypeStruct((acc.shape[0] // 2, PAIR), jnp.bfloat16),
        in_specs=[VMEM] * 3,
        out_specs=VMEM,
        compiler_params=pltpu.CompilerParams(vmem_limit_bytes=12 * 2**20),
        cost_estimate=pl.CostEstimate(flops=0, bytes_accessed=2**20, transcendentals=0),
    )(acc, top, sent)


def unpack_kernel(main, *refs):
    extra, out = refs[:4], refs[4]

    def put(block, lanes):
        out[:Q_ROWS, lanes] = block[:, :HEAD_DIM]
        out[Q_ROWS:, lanes] = block[:, HEAD_DIM:]

    for head in range(COLUMNS):
        put(main.at[head], pl.ds(head * HEAD_DIM, HEAD_DIM))
    x = lax.axis_index("x")
    for step, block in zip((0, *STEPS), extra, strict=True):
        head = COLUMNS + lax.rem(x + step, 4)
        put(block, pl.ds(pl.multiple_of(head * HEAD_DIM, HEAD_DIM), HEAD_DIM))


def unpack(main, extra):
    return pl.pallas_call(
        unpack_kernel,
        out_shape=jax.ShapeDtypeStruct((TOKENS, HEADS * HEAD_DIM), jnp.bfloat16),
        in_specs=[VMEM] * 5,
        out_specs=VMEM,
        compiler_params=pltpu.CompilerParams(vmem_limit_bytes=8 * 2**20),
        cost_estimate=pl.CostEstimate(flops=0, bytes_accessed=2**20, transcendentals=0),
    )(main, *extra)


def local(queries, keys, values):
    arrays = (queries, keys, values)
    rows = KV_ROWS + Q_ROWS
    extra = packed(pack_extra_kernel, arrays, [(rows, PAIR)] * 4, EXTRA * HEAD_DIM, 60)
    (sent,) = packed(pack_main_kernel, arrays, [(COLUMNS, rows, PAIR)], COLUMNS * HEAD_DIM, 12)

    extra = [extra[0]] + [along("x", a, step) for a, step in zip(extra[1:], STEPS, strict=True)]
    xkv, xq = gather(extra)
    xqs = [xq] + [along("y", xq, step) for step in STEPS]
    xkvs = [xkv, along_z(xkv, 1), along_z(xkv, 3)]
    xkvs.append(along_z(xkvs[1], 1))

    got = lax.all_to_all(sent, ("x", "y"), 0, 0, tiled=True)
    kv, q = sort(got)
    near = key_partner(kv)
    near_q = query_partner(q)
    both, xq = stack(kv, *xkvs), stack(*xqs, flops=2 * 10**10)
    other = other_core(both)

    rows = kv.shape[0]
    parts = attend(xq, [both[rows:], other[rows:]], None, "part")
    back = [along("y", part, -step) for part, step in zip(parts[1:], STEPS, strict=True)]
    xout = combine([parts[0], *back])

    near = hold(near, parts[0])
    near_other = other_core(near)
    state = attend(near_q, [kv, other[:rows]], None, None, (near,), flops=2 * 10**10)
    sent = attend(near_q, [near, near_other], state, "send", back)
    state = attend(q, [kv, other[:rows], near, near_other], None, None, (sent, xout[0]))
    out = merge(*state, query_partner(sent))
    out = lax.all_to_all(out.reshape(COLUMNS, Q_ROWS, PAIR), ("x", "y"), 0, 0, tiled=True)
    xout = [xout[0]] + [along("x", a, -step) for a, step in zip(xout[1:], STEPS, strict=True)]
    return unpack(out, xout)


def solution(mesh):
    fine = Mesh(mesh.devices.reshape(SIZES), AXES)
    return jax.shard_map(
        local, mesh=fine, in_specs=(P(AXES, None),) * 3, out_specs=P(AXES, None), check_vma=False
    )
```

```python
import functools

import jax
import jax.numpy as jnp
from jax import lax
from jax.experimental import pallas as pl
from jax.experimental.pallas import tpu as pltpu
from jax.sharding import Mesh, PartitionSpec as P

HEADS = 20
HEAD_DIM = 128
PAIR = 2 * HEAD_DIM
SCALE = HEAD_DIM**-0.5 * 1.4426950408889634
AXES = ("x", "zl", "y", "zh", "c")
SIZES = (4, 2, 4, 2, 2)
COLUMNS = 16
TOKENS = 80
EXTRA = HEADS - COLUMNS
K_BLOCK = 256
CODE_ROWS = 16
STEPS = (1, 3, 2)
NT = (((1,), (1,)), ((), ()))
KV_ROWS, Q_ROWS = TOKENS, TOKENS // 2
VMEM = pl.BlockSpec(memory_space=pltpu.VMEM)
HBM = pl.BlockSpec(memory_space=pltpu.HBM)


def along_z(a, step):
    pairs = []
    for zl in range(2):
        for zh in range(2):
            z = (2 * zh + zl + step) % 4
            pairs.append((2 * zl + zh, 2 * (z % 2) + z // 2))
    return lax.ppermute(a, ("zl", "zh"), pairs)


def along(axis, a, step):
    return lax.ppermute(a, axis, [(i, (i + step) % 4) for i in range(4)])


def key_partner(a):
    return lax.ppermute(a, "zl", [(0, 1), (1, 0)])


def query_partner(a):
    return lax.ppermute(a, ("zl", "zh"), [(0, 3), (3, 0), (1, 2), (2, 1)])


def other_core(a):
    return lax.ppermute(a, "c", [(0, 1), (1, 0)])


def scaled_halves(q):
    full = q.astype(jnp.float32) * SCALE
    high = full.astype(jnp.bfloat16)
    low = (full - high.astype(jnp.float32)).astype(jnp.bfloat16)
    return jnp.concatenate([high, low], axis=1)


def diagonal():
    shape = (HEAD_DIM, HEAD_DIM)
    return lax.broadcasted_iota(jnp.int32, shape, 0) == lax.broadcasted_iota(jnp.int32, shape, 1)


def coded_rows(level):
    blocks = level.shape[0] // HEAD_DIM
    row = lax.broadcasted_iota(jnp.int32, (CODE_ROWS, HEAD_DIM), 0)
    coded = jnp.zeros((CODE_ROWS, HEAD_DIM), jnp.float32)
    for i in range(blocks):
        block = jnp.where(diagonal(), level[i * HEAD_DIM : (i + 1) * HEAD_DIM, :], 0.0)
        rest = jnp.sum(block, axis=0, keepdims=True)
        for term in range(3):
            rounded = rest.astype(jnp.bfloat16).astype(jnp.float32)
            coded = jnp.where(row == term * blocks + i, rounded, coded)
            rest = rest - rounded
    return coded


def decoded_column(coded, i, blocks):
    row = lax.broadcasted_iota(jnp.int32, coded.shape, 0)
    mine = (row == i) | (row == blocks + i) | (row == 2 * blocks + i)
    numbers = jnp.sum(jnp.where(mine, coded, 0.0), axis=0, keepdims=True)
    return jnp.sum(jnp.where(diagonal(), numbers, 0.0), axis=1, keepdims=True)


def attend_kernel(n_kv, n_after, first, last, *refs):
    refs = list(refs)
    q_ref, kv_refs, refs = refs[0], refs[1 : 1 + n_kv], refs[1 + n_kv :]
    if not first:
        acc_in, top_in = refs[:2]
        refs = refs[2:]
    refs = refs[n_after:]
    rows = q_ref.shape[0]
    ones = jnp.ones((K_BLOCK, HEAD_DIM), jnp.bfloat16)
    q = jnp.concatenate([scaled_halves(q_ref[:, :HEAD_DIM]), scaled_halves(q_ref[:, HEAD_DIM:])], axis=0)
    if first:
        top = jnp.full((2 * rows, 1), -1e30, jnp.float32)
        acc = jnp.zeros((2 * rows, PAIR), jnp.float32)
    else:
        top = jnp.max(top_in[...], axis=1, keepdims=True)
        acc = acc_in[...]
    for kv_ref in kv_refs:
        for j in range(kv_ref.shape[0] // K_BLOCK):
            there = slice(j * K_BLOCK, (j + 1) * K_BLOCK)
            k = kv_ref[there, :HEAD_DIM]
            v = kv_ref[there, HEAD_DIM:]
            scores = lax.dot_general(
                q, jnp.concatenate([k, k], axis=1), NT, preferred_element_type=jnp.float32
            )
            fresh = jnp.maximum(top, jnp.max(scores, axis=1, keepdims=True))
            weights = jnp.exp2(scores - fresh).astype(jnp.bfloat16)
            acc = acc * jnp.exp2(top - fresh) + jnp.dot(
                weights, jnp.concatenate([v, ones], axis=1), preferred_element_type=jnp.float32
            )
            top = fresh
    whole_top, whole_acc = top, acc
    for half in range(2):
        lanes = slice(half * HEAD_DIM, (half + 1) * HEAD_DIM)
        here = slice(half * rows, (half + 1) * rows)
        top, acc = whole_top[here, :], whole_acc[here, :]
        if last == "send":
            total = acc[:, HEAD_DIM:]
            refs[0][:rows, lanes] = (acc[:, :HEAD_DIM] / total).astype(jnp.bfloat16)
            refs[0][rows:, lanes] = coded_rows(top + jnp.log2(total)).astype(jnp.bfloat16)
        elif last == "part":
            total = acc[:, HEAD_DIM:]
            part = (acc[:, :HEAD_DIM] / total).astype(jnp.bfloat16)
            coded = coded_rows(top + jnp.log2(total)).astype(jnp.bfloat16)
            some = rows // 4
            for i, ref in enumerate(refs):
                ref[:some, lanes] = part[i * some : (i + 1) * some, :]
                ref[some:, lanes] = coded
        else:
            refs[0][here, :] = acc
            refs[1][here, :] = jnp.broadcast_to(top, (rows, HEAD_DIM))


def attend(q, kvs, state, last, after=(), flops=0):
    rows = q.shape[0]
    keys = sum(kv.shape[0] for kv in kvs)
    if last is None:
        out_shape = (
            jax.ShapeDtypeStruct((2 * rows, PAIR), jnp.float32),
            jax.ShapeDtypeStruct((2 * rows, HEAD_DIM), jnp.float32),
        )
    elif last == "part":
        out_shape = (jax.ShapeDtypeStruct((rows // 4 + CODE_ROWS, PAIR), jnp.bfloat16),) * 4
    else:
        out_shape = (jax.ShapeDtypeStruct((rows + CODE_ROWS, PAIR), jnp.bfloat16),)
    args = (q, *kvs, *(state or ()))
    result = pl.pallas_call(
        functools.partial(attend_kernel, len(kvs), len(after), state is None, last),
        out_shape=out_shape,
        in_specs=[VMEM] * len(args) + [HBM] * len(after),
        out_specs=(VMEM,) * len(out_shape),
        compiler_params=pltpu.CompilerParams(vmem_limit_bytes=20 * 2**20),
        cost_estimate=pl.CostEstimate(
            flops=flops, bytes_accessed=4 * keys * HEAD_DIM, transcendentals=0
        ),
    )(*args, *after)
    return result[0] if last == "send" else result


def combine_kernel(*refs):
    parts, outs = refs[:4], refs[4:]
    rows = parts[0].shape[0] - CODE_ROWS
    blocks = 4 * rows // HEAD_DIM
    for half in range(2):
        lanes = slice(half * HEAD_DIM, (half + 1) * HEAD_DIM)
        levels = []
        for i, part in enumerate(parts):
            first, start = divmod(i * rows, HEAD_DIM)
            coded = part[rows:, lanes].astype(jnp.float32)
            column = jnp.concatenate([decoded_column(coded, first + j, blocks) for j in range(2)], axis=0)
            levels.append(column[start : start + rows, :])
        top = functools.reduce(jnp.maximum, levels)
        shares = [jnp.exp2(level - top) for level in levels]
        total = functools.reduce(jnp.add, shares)
        summed = functools.reduce(
            jnp.add, [share * p[:rows, lanes].astype(jnp.float32) for share, p in zip(shares, parts, strict=True)]
        )
        whole = (summed / total).astype(jnp.bfloat16)
        for i, out in enumerate(outs):
            out[:, lanes] = whole[i * Q_ROWS : (i + 1) * Q_ROWS, :]


def combine(parts):
    rows = parts[0].shape[0]
    return pl.pallas_call(
        combine_kernel,
        out_shape=[jax.ShapeDtypeStruct((Q_ROWS, PAIR), jnp.bfloat16)] * 4,
        in_specs=[VMEM] * 4,
        out_specs=[VMEM] * 4,
        compiler_params=pltpu.CompilerParams(vmem_limit_bytes=8 * 2**20),
        cost_estimate=pl.CostEstimate(flops=16 * rows * PAIR, bytes_accessed=16 * rows * PAIR, transcendentals=0),
    )(*parts)


def fetch(sources, first, scratch, sems):
    copies = [
        pltpu.make_async_copy(source.at[:, pl.ds(first, held.shape[1])], held, sems.at[i])
        for i, (source, held) in enumerate(zip(sources, scratch, strict=True))
    ]
    for copy in copies:
        copy.start()
    for copy in copies:
        copy.wait()


def pack(out, q_ref, k_ref, v_ref, lanes):
    out[:KV_ROWS, :HEAD_DIM] = k_ref[:, lanes]
    out[:KV_ROWS, HEAD_DIM:] = v_ref[:, lanes]
    out[KV_ROWS:, :HEAD_DIM] = q_ref[:Q_ROWS, lanes]
    out[KV_ROWS:, HEAD_DIM:] = q_ref[Q_ROWS:, lanes]


def pack_extra_kernel(*refs):
    sources, outs, scratch, sems = refs[:3], refs[3:7], refs[7:10], refs[10]
    fetch(sources, COLUMNS * HEAD_DIM, scratch, sems)
    x = lax.axis_index("x")
    for step, out in zip((0, *STEPS), outs, strict=True):
        head = lax.rem(x + step, 4)
        pack(out, *scratch, pl.ds(pl.multiple_of(head * HEAD_DIM, HEAD_DIM), HEAD_DIM))


def pack_main_kernel(*refs):
    sources, out, scratch, sems = refs[:3], refs[3], refs[4:7], refs[7]
    fetch(sources, 0, scratch, sems)
    for head in range(COLUMNS):
        pack(out.at[head], *scratch, pl.ds(head * HEAD_DIM, HEAD_DIM))


def packed(kernel, arrays, shapes, columns, grant):
    return pl.pallas_call(
        kernel,
        out_shape=[jax.ShapeDtypeStruct(shape, jnp.bfloat16) for shape in shapes],
        in_specs=[HBM] * 3,
        out_specs=[VMEM] * len(shapes),
        scratch_shapes=[pltpu.VMEM((TOKENS, columns), jnp.bfloat16)] * 3 + [pltpu.SemaphoreType.DMA((3,))],
        compiler_params=pltpu.CompilerParams(vmem_limit_bytes=grant * 2**20),
        cost_estimate=pl.CostEstimate(flops=0, bytes_accessed=2**20, transcendentals=0),
    )(*arrays)


def gather_kernel(*refs):
    pieces, xkv, xq = refs[:4], refs[4], refs[5]
    for i, piece in enumerate(pieces):
        xkv[i * KV_ROWS : (i + 1) * KV_ROWS, :] = piece[:KV_ROWS, :]
        xq[i * Q_ROWS : (i + 1) * Q_ROWS, :] = piece[KV_ROWS:, :]


def gather(pieces):
    return pl.pallas_call(
        gather_kernel,
        out_shape=[jax.ShapeDtypeStruct((4 * rows, PAIR), jnp.bfloat16) for rows in (KV_ROWS, Q_ROWS)],
        in_specs=[VMEM] * 4,
        out_specs=[VMEM] * 2,
        compiler_params=pltpu.CompilerParams(vmem_limit_bytes=8 * 2**20),
        cost_estimate=pl.CostEstimate(flops=2 * 10**10, bytes_accessed=2**20, transcendentals=0),
    )(*pieces)


def sort_kernel(got, kv, q):
    for i in range(COLUMNS):
        kv[i * KV_ROWS : (i + 1) * KV_ROWS, :] = got[i, :KV_ROWS, :]
        q[i * Q_ROWS : (i + 1) * Q_ROWS, :] = got[i, KV_ROWS:, :]


def sort(got):
    return pl.pallas_call(
        sort_kernel,
        out_shape=[jax.ShapeDtypeStruct((COLUMNS * rows, PAIR), jnp.bfloat16) for rows in (KV_ROWS, Q_ROWS)],
        in_specs=[VMEM],
        out_specs=[VMEM] * 2,
        compiler_params=pltpu.CompilerParams(vmem_limit_bytes=12 * 2**20),
        cost_estimate=pl.CostEstimate(flops=0, bytes_accessed=2**20, transcendentals=0),
    )(got)


def stack_kernel(*refs):
    out, start = refs[-1], 0
    for ref in refs[:-1]:
        out[start : start + ref.shape[0], :] = ref[...]
        start += ref.shape[0]


def stack(*pieces, flops=0):
    return pl.pallas_call(
        stack_kernel,
        out_shape=jax.ShapeDtypeStruct((sum(piece.shape[0] for piece in pieces), PAIR), jnp.bfloat16),
        in_specs=[VMEM] * len(pieces),
        out_specs=VMEM,
        compiler_params=pltpu.CompilerParams(vmem_limit_bytes=12 * 2**20),
        cost_estimate=pl.CostEstimate(flops=flops, bytes_accessed=2**20, transcendentals=0),
    )(*pieces)


def hold_kernel(a, *refs):
    refs[-1][...] = a[...]


def hold(a, *after):
    return pl.pallas_call(
        hold_kernel,
        out_shape=jax.ShapeDtypeStruct(a.shape, a.dtype),
        in_specs=[VMEM] + [HBM] * len(after),
        out_specs=VMEM,
        compiler_params=pltpu.CompilerParams(vmem_limit_bytes=12 * 2**20),
        cost_estimate=pl.CostEstimate(flops=0, bytes_accessed=2**20, transcendentals=0),
    )(a, *after)


def merge_kernel(acc, top, sent, out):
    rows = out.shape[0]
    blocks = rows // HEAD_DIM
    for half in range(2):
        lanes = slice(half * HEAD_DIM, (half + 1) * HEAD_DIM)
        coded = sent[rows:, lanes].astype(jnp.float32)
        for i in range(blocks):
            there = slice(i * HEAD_DIM, (i + 1) * HEAD_DIM)
            here = slice(half * rows + i * HEAD_DIM, half * rows + (i + 1) * HEAD_DIM)
            other = decoded_column(coded, i, blocks)
            largest = jnp.maximum(top[here, :], other)
            share, other = jnp.exp2(top[here, :] - largest), jnp.exp2(other - largest)
            summed = acc[here, :HEAD_DIM] * share + sent[there, lanes].astype(jnp.float32) * other
            out[there, lanes] = (summed / (acc[here, HEAD_DIM:] * share + other)).astype(jnp.bfloat16)


def merge(acc, top, sent):
    return pl.pallas_call(
        merge_kernel,
        out_shape=jax.ShapeDtypeStruct((acc.shape[0] // 2, PAIR), jnp.bfloat16),
        in_specs=[VMEM] * 3,
        out_specs=VMEM,
        compiler_params=pltpu.CompilerParams(vmem_limit_bytes=12 * 2**20),
        cost_estimate=pl.CostEstimate(flops=0, bytes_accessed=2**20, transcendentals=0),
    )(acc, top, sent)


def unpack_kernel(main, *refs):
    extra, out = refs[:4], refs[4]

    def put(block, lanes):
        out[:Q_ROWS, lanes] = block[:, :HEAD_DIM]
        out[Q_ROWS:, lanes] = block[:, HEAD_DIM:]

    for head in range(COLUMNS):
        put(main.at[head], pl.ds(head * HEAD_DIM, HEAD_DIM))
    x = lax.axis_index("x")
    for step, block in zip((0, *STEPS), extra, strict=True):
        head = COLUMNS + lax.rem(x + step, 4)
        put(block, pl.ds(pl.multiple_of(head * HEAD_DIM, HEAD_DIM), HEAD_DIM))


def unpack(main, extra):
    return pl.pallas_call(
        unpack_kernel,
        out_shape=jax.ShapeDtypeStruct((TOKENS, HEADS * HEAD_DIM), jnp.bfloat16),
        in_specs=[VMEM] * 5,
        out_specs=VMEM,
        compiler_params=pltpu.CompilerParams(vmem_limit_bytes=8 * 2**20),
        cost_estimate=pl.CostEstimate(flops=0, bytes_accessed=2**20, transcendentals=0),
    )(main, *extra)


def local(queries, keys, values):
    arrays = (queries, keys, values)
    rows = KV_ROWS + Q_ROWS
    extra = packed(pack_extra_kernel, arrays, [(rows, PAIR)] * 4, EXTRA * HEAD_DIM, 60)
    (sent,) = packed(pack_main_kernel, arrays, [(COLUMNS, rows, PAIR)], COLUMNS * HEAD_DIM, 12)

    extra = [extra[0]] + [along("x", a, step) for a, step in zip(extra[1:], STEPS, strict=True)]
    xkv, xq = gather(extra)
    xqs = [xq] + [along("y", xq, step) for step in STEPS]
    xkvs = [xkv, along_z(xkv, 1), along_z(xkv, 3)]
    xkvs.append(along_z(xkvs[1], 1))

    got = lax.all_to_all(sent, ("x", "y"), 0, 0, tiled=True)
    kv, q = sort(got)
    near = key_partner(kv)
    near_q = query_partner(q)
    both, xq = stack(kv, *xkvs), stack(*xqs, flops=2 * 10**10)
    other = other_core(both)

    rows = kv.shape[0]
    parts = attend(xq, [both[rows:], other[rows:]], None, "part")
    back = [along("y", part, -step) for part, step in zip(parts[1:], STEPS, strict=True)]
    xout = combine([parts[0], *back])

    near = hold(near, parts[0])
    near_other = other_core(near)
    state = attend(near_q, [kv, other[:rows]], None, None, (near,), flops=2 * 10**10)
    sent = attend(near_q, [near, near_other], state, "send", back)
    state = attend(q, [kv, other[:rows], near, near_other], None, None, (sent, xout[0]))
    out = merge(*state, query_partner(sent))
    out = lax.all_to_all(out.reshape(COLUMNS, Q_ROWS, PAIR), ("x", "y"), 0, 0, tiled=True)
    xout = [xout[0]] + [along("x", a, -step) for a, step in zip(xout[1:], STEPS, strict=True)]
    return unpack(out, xout)


def solution(mesh):
    fine = Mesh(mesh.devices.reshape(SIZES), AXES)
    return jax.shard_map(
        local, mesh=fine, in_specs=(P(AXES, None),) * 3, out_specs=P(AXES, None), check_vma=False
    )
```

```python
import functools

import jax
import jax.numpy as jnp
from jax import lax
from jax.experimental import pallas as pl
from jax.experimental.pallas import tpu as pltpu
from jax.sharding import Mesh, PartitionSpec as P

HEADS = 20
HEAD_DIM = 128
PAIR = 2 * HEAD_DIM
SCALE = HEAD_DIM**-0.5 * 1.4426950408889634
AXES = ("x", "zl", "y", "zh", "c")
SIZES = (4, 2, 4, 2, 2)
COLUMNS = 16
TOKENS = 80
EXTRA = HEADS - COLUMNS
K_BLOCK = 256
CODE_ROWS = 16
STEPS = (1, 3, 2)
NT = (((1,), (1,)), ((), ()))
KV_ROWS, Q_ROWS = TOKENS, TOKENS // 2
VMEM = pl.BlockSpec(memory_space=pltpu.VMEM)
HBM = pl.BlockSpec(memory_space=pltpu.HBM)


def along_z(a, step):
    pairs = []
    for zl in range(2):
        for zh in range(2):
            z = (2 * zh + zl + step) % 4
            pairs.append((2 * zl + zh, 2 * (z % 2) + z // 2))
    return lax.ppermute(a, ("zl", "zh"), pairs)


def along(axis, a, step):
    return lax.ppermute(a, axis, [(i, (i + step) % 4) for i in range(4)])


def key_partner(a):
    return lax.ppermute(a, "zl", [(0, 1), (1, 0)])


def query_partner(a):
    return lax.ppermute(a, ("zl", "zh"), [(0, 3), (3, 0), (1, 2), (2, 1)])


def other_core(a):
    return lax.ppermute(a, "c", [(0, 1), (1, 0)])


def scaled_halves(q):
    full = q.astype(jnp.float32) * SCALE
    high = full.astype(jnp.bfloat16)
    low = (full - high.astype(jnp.float32)).astype(jnp.bfloat16)
    return jnp.concatenate([high, low], axis=1)


def diagonal():
    shape = (HEAD_DIM, HEAD_DIM)
    return lax.broadcasted_iota(jnp.int32, shape, 0) == lax.broadcasted_iota(jnp.int32, shape, 1)


def coded_rows(level):
    blocks = level.shape[0] // HEAD_DIM
    row = lax.broadcasted_iota(jnp.int32, (CODE_ROWS, HEAD_DIM), 0)
    coded = jnp.zeros((CODE_ROWS, HEAD_DIM), jnp.float32)
    for i in range(blocks):
        block = jnp.where(diagonal(), level[i * HEAD_DIM : (i + 1) * HEAD_DIM, :], 0.0)
        rest = jnp.sum(block, axis=0, keepdims=True)
        for term in range(3):
            rounded = rest.astype(jnp.bfloat16).astype(jnp.float32)
            coded = jnp.where(row == term * blocks + i, rounded, coded)
            rest = rest - rounded
    return coded


def decoded_column(coded, i, blocks):
    row = lax.broadcasted_iota(jnp.int32, coded.shape, 0)
    mine = (row == i) | (row == blocks + i) | (row == 2 * blocks + i)
    numbers = jnp.sum(jnp.where(mine, coded, 0.0), axis=0, keepdims=True)
    return jnp.sum(jnp.where(diagonal(), numbers, 0.0), axis=1, keepdims=True)


def attend_kernel(n_kv, n_after, first, last, *refs):
    refs = list(refs)
    q_ref, kv_refs, refs = refs[0], refs[1 : 1 + n_kv], refs[1 + n_kv :]
    if not first:
        acc_in, top_in = refs[:2]
        refs = refs[2:]
    refs = refs[n_after:]
    rows = q_ref.shape[0]
    ones = jnp.ones((K_BLOCK, HEAD_DIM), jnp.bfloat16)
    q = jnp.concatenate([scaled_halves(q_ref[:, :HEAD_DIM]), scaled_halves(q_ref[:, HEAD_DIM:])], axis=0)
    if first:
        top = jnp.full((2 * rows, 1), -1e30, jnp.float32)
        acc = jnp.zeros((2 * rows, PAIR), jnp.float32)
    else:
        top = jnp.max(top_in[...], axis=1, keepdims=True)
        acc = acc_in[...]
    for kv_ref in kv_refs:
        for j in range(kv_ref.shape[0] // K_BLOCK):
            there = slice(j * K_BLOCK, (j + 1) * K_BLOCK)
            k = kv_ref[there, :HEAD_DIM]
            v = kv_ref[there, HEAD_DIM:]
            scores = lax.dot_general(
                q, jnp.concatenate([k, k], axis=1), NT, preferred_element_type=jnp.float32
            )
            fresh = jnp.maximum(top, jnp.max(scores, axis=1, keepdims=True))
            weights = jnp.exp2(scores - fresh).astype(jnp.bfloat16)
            acc = acc * jnp.exp2(top - fresh) + jnp.dot(
                weights, jnp.concatenate([v, ones], axis=1), preferred_element_type=jnp.float32
            )
            top = fresh
    whole_top, whole_acc = top, acc
    for half in range(2):
        lanes = slice(half * HEAD_DIM, (half + 1) * HEAD_DIM)
        here = slice(half * rows, (half + 1) * rows)
        top, acc = whole_top[here, :], whole_acc[here, :]
        if last == "send":
            total = acc[:, HEAD_DIM:]
            refs[0][:rows, lanes] = (acc[:, :HEAD_DIM] / total).astype(jnp.bfloat16)
            refs[0][rows:, lanes] = coded_rows(top + jnp.log2(total)).astype(jnp.bfloat16)
        elif last == "part":
            total = acc[:, HEAD_DIM:]
            part = (acc[:, :HEAD_DIM] / total).astype(jnp.bfloat16)
            coded = coded_rows(top + jnp.log2(total)).astype(jnp.bfloat16)
            some = rows // 4
            for i, ref in enumerate(refs):
                ref[:some, lanes] = part[i * some : (i + 1) * some, :]
                ref[some:, lanes] = coded
        else:
            refs[0][here, :] = acc
            refs[1][here, :] = jnp.broadcast_to(top, (rows, HEAD_DIM))


def attend(q, kvs, state, last, after=(), flops=0):
    rows = q.shape[0]
    keys = sum(kv.shape[0] for kv in kvs)
    if last is None:
        out_shape = (
            jax.ShapeDtypeStruct((2 * rows, PAIR), jnp.float32),
            jax.ShapeDtypeStruct((2 * rows, HEAD_DIM), jnp.float32),
        )
    elif last == "part":
        out_shape = (jax.ShapeDtypeStruct((rows // 4 + CODE_ROWS, PAIR), jnp.bfloat16),) * 4
    else:
        out_shape = (jax.ShapeDtypeStruct((rows + CODE_ROWS, PAIR), jnp.bfloat16),)
    args = (q, *kvs, *(state or ()))
    result = pl.pallas_call(
        functools.partial(attend_kernel, len(kvs), len(after), state is None, last),
        out_shape=out_shape,
        in_specs=[VMEM] * len(args) + [HBM] * len(after),
        out_specs=(VMEM,) * len(out_shape),
        compiler_params=pltpu.CompilerParams(vmem_limit_bytes=20 * 2**20),
        cost_estimate=pl.CostEstimate(
            flops=flops, bytes_accessed=4 * keys * HEAD_DIM, transcendentals=0
        ),
    )(*args, *after)
    return result[0] if last == "send" else result


def combine_kernel(*refs):
    parts, outs = refs[:4], refs[4:]
    rows = parts[0].shape[0] - CODE_ROWS
    blocks = 4 * rows // HEAD_DIM
    for half in range(2):
        lanes = slice(half * HEAD_DIM, (half + 1) * HEAD_DIM)
        levels = []
        for i, part in enumerate(parts):
            first, start = divmod(i * rows, HEAD_DIM)
            coded = part[rows:, lanes].astype(jnp.float32)
            column = jnp.concatenate([decoded_column(coded, first + j, blocks) for j in range(2)], axis=0)
            levels.append(column[start : start + rows, :])
        top = functools.reduce(jnp.maximum, levels)
        shares = [jnp.exp2(level - top) for level in levels]
        total = functools.reduce(jnp.add, shares)
        summed = functools.reduce(
            jnp.add, [share * p[:rows, lanes].astype(jnp.float32) for share, p in zip(shares, parts, strict=True)]
        )
        whole = (summed / total).astype(jnp.bfloat16)
        for i, out in enumerate(outs):
            out[:, lanes] = whole[i * Q_ROWS : (i + 1) * Q_ROWS, :]


def combine(parts):
    rows = parts[0].shape[0]
    return pl.pallas_call(
        combine_kernel,
        out_shape=[jax.ShapeDtypeStruct((Q_ROWS, PAIR), jnp.bfloat16)] * 4,
        in_specs=[VMEM] * 4,
        out_specs=[VMEM] * 4,
        compiler_params=pltpu.CompilerParams(vmem_limit_bytes=8 * 2**20),
        cost_estimate=pl.CostEstimate(flops=16 * rows * PAIR, bytes_accessed=16 * rows * PAIR, transcendentals=0),
    )(*parts)


def fetch(sources, first, scratch, sems):
    copies = [
        pltpu.make_async_copy(source.at[:, pl.ds(first, held.shape[1])], held, sems.at[i])
        for i, (source, held) in enumerate(zip(sources, scratch, strict=True))
    ]
    for copy in copies:
        copy.start()
    for copy in copies:
        copy.wait()


def pack(out, q_ref, k_ref, v_ref, lanes):
    out[:KV_ROWS, :HEAD_DIM] = k_ref[:, lanes]
    out[:KV_ROWS, HEAD_DIM:] = v_ref[:, lanes]
    out[KV_ROWS:, :HEAD_DIM] = q_ref[:Q_ROWS, lanes]
    out[KV_ROWS:, HEAD_DIM:] = q_ref[Q_ROWS:, lanes]


def pack_extra_kernel(*refs):
    sources, outs, scratch, sems = refs[:3], refs[3:7], refs[7:10], refs[10]
    fetch(sources, COLUMNS * HEAD_DIM, scratch, sems)
    x = lax.axis_index("x")
    for step, out in zip((0, *STEPS), outs, strict=True):
        head = lax.rem(x + step, 4)
        pack(out, *scratch, pl.ds(pl.multiple_of(head * HEAD_DIM, HEAD_DIM), HEAD_DIM))


def pack_main_kernel(*refs):
    sources, out, scratch, sems = refs[:3], refs[3], refs[4:7], refs[7]
    fetch(sources, 0, scratch, sems)
    for head in range(COLUMNS):
        pack(out.at[head], *scratch, pl.ds(head * HEAD_DIM, HEAD_DIM))


def packed(kernel, arrays, shapes, columns, grant):
    return pl.pallas_call(
        kernel,
        out_shape=[jax.ShapeDtypeStruct(shape, jnp.bfloat16) for shape in shapes],
        in_specs=[HBM] * 3,
        out_specs=[VMEM] * len(shapes),
        scratch_shapes=[pltpu.VMEM((TOKENS, columns), jnp.bfloat16)] * 3 + [pltpu.SemaphoreType.DMA((3,))],
        compiler_params=pltpu.CompilerParams(vmem_limit_bytes=grant * 2**20),
        cost_estimate=pl.CostEstimate(flops=0, bytes_accessed=2**20, transcendentals=0),
    )(*arrays)


def gather_kernel(*refs):
    pieces, xkv, xq = refs[:4], refs[4], refs[5]
    for i, piece in enumerate(pieces):
        xkv[i * KV_ROWS : (i + 1) * KV_ROWS, :] = piece[:KV_ROWS, :]
        xq[i * Q_ROWS : (i + 1) * Q_ROWS, :] = piece[KV_ROWS:, :]


def gather(pieces):
    return pl.pallas_call(
        gather_kernel,
        out_shape=[jax.ShapeDtypeStruct((4 * rows, PAIR), jnp.bfloat16) for rows in (KV_ROWS, Q_ROWS)],
        in_specs=[VMEM] * 4,
        out_specs=[VMEM] * 2,
        compiler_params=pltpu.CompilerParams(vmem_limit_bytes=8 * 2**20),
        cost_estimate=pl.CostEstimate(flops=2 * 10**10, bytes_accessed=2**20, transcendentals=0),
    )(*pieces)


def sort_kernel(got, kv, q):
    for i in range(COLUMNS):
        kv[i * KV_ROWS : (i + 1) * KV_ROWS, :] = got[i, :KV_ROWS, :]
        q[i * Q_ROWS : (i + 1) * Q_ROWS, :] = got[i, KV_ROWS:, :]


def sort(got):
    return pl.pallas_call(
        sort_kernel,
        out_shape=[jax.ShapeDtypeStruct((COLUMNS * rows, PAIR), jnp.bfloat16) for rows in (KV_ROWS, Q_ROWS)],
        in_specs=[VMEM],
        out_specs=[VMEM] * 2,
        compiler_params=pltpu.CompilerParams(vmem_limit_bytes=12 * 2**20),
        cost_estimate=pl.CostEstimate(flops=0, bytes_accessed=2**20, transcendentals=0),
    )(got)


def stack_kernel(*refs):
    out, start = refs[-1], 0
    for ref in refs[:-1]:
        if start < out.shape[0]:
            out[start : start + ref.shape[0], :] = ref[...]
            start += ref.shape[0]


def stack(*pieces, after=(), flops=0):
    return pl.pallas_call(
        stack_kernel,
        out_shape=jax.ShapeDtypeStruct((sum(piece.shape[0] for piece in pieces), PAIR), jnp.bfloat16),
        in_specs=[VMEM] * len(pieces) + [HBM] * len(after),
        out_specs=VMEM,
        compiler_params=pltpu.CompilerParams(vmem_limit_bytes=12 * 2**20),
        cost_estimate=pl.CostEstimate(flops=flops, bytes_accessed=2**20, transcendentals=0),
    )(*pieces, *after)


def hold_kernel(a, *refs):
    refs[-1][...] = a[...]


def hold(a, *after):
    return pl.pallas_call(
        hold_kernel,
        out_shape=jax.ShapeDtypeStruct(a.shape, a.dtype),
        in_specs=[VMEM] + [HBM] * len(after),
        out_specs=VMEM,
        compiler_params=pltpu.CompilerParams(vmem_limit_bytes=12 * 2**20),
        cost_estimate=pl.CostEstimate(flops=0, bytes_accessed=2**20, transcendentals=0),
    )(a, *after)


def merge_kernel(acc, top, sent, *refs):
    out = refs[-1]
    rows = out.shape[0]
    blocks = rows // HEAD_DIM
    for half in range(2):
        lanes = slice(half * HEAD_DIM, (half + 1) * HEAD_DIM)
        coded = sent[rows:, lanes].astype(jnp.float32)
        for i in range(blocks):
            there = slice(i * HEAD_DIM, (i + 1) * HEAD_DIM)
            here = slice(half * rows + i * HEAD_DIM, half * rows + (i + 1) * HEAD_DIM)
            other = decoded_column(coded, i, blocks)
            largest = jnp.maximum(top[here, :], other)
            share, other = jnp.exp2(top[here, :] - largest), jnp.exp2(other - largest)
            summed = acc[here, :HEAD_DIM] * share + sent[there, lanes].astype(jnp.float32) * other
            out[there, lanes] = (summed / (acc[here, HEAD_DIM:] * share + other)).astype(jnp.bfloat16)


def merge(acc, top, sent, *after):
    return pl.pallas_call(
        merge_kernel,
        out_shape=jax.ShapeDtypeStruct((acc.shape[0] // 2, PAIR), jnp.bfloat16),
        in_specs=[VMEM] * 3 + [HBM] * len(after),
        out_specs=VMEM,
        compiler_params=pltpu.CompilerParams(vmem_limit_bytes=12 * 2**20),
        cost_estimate=pl.CostEstimate(flops=0, bytes_accessed=2**20, transcendentals=0),
    )(acc, top, sent, *after)


def unpack_kernel(main, *refs):
    extra, out = refs[:4], refs[4]

    def put(block, lanes):
        out[:Q_ROWS, lanes] = block[:, :HEAD_DIM]
        out[Q_ROWS:, lanes] = block[:, HEAD_DIM:]

    for head in range(COLUMNS):
        put(main.at[head], pl.ds(head * HEAD_DIM, HEAD_DIM))
    x = lax.axis_index("x")
    for step, block in zip((0, *STEPS), extra, strict=True):
        head = COLUMNS + lax.rem(x + step, 4)
        put(block, pl.ds(pl.multiple_of(head * HEAD_DIM, HEAD_DIM), HEAD_DIM))


def unpack(main, extra):
    return pl.pallas_call(
        unpack_kernel,
        out_shape=jax.ShapeDtypeStruct((TOKENS, HEADS * HEAD_DIM), jnp.bfloat16),
        in_specs=[VMEM] * 5,
        out_specs=VMEM,
        compiler_params=pltpu.CompilerParams(vmem_limit_bytes=8 * 2**20),
        cost_estimate=pl.CostEstimate(flops=0, bytes_accessed=2**20, transcendentals=0),
    )(main, *extra)


def local(queries, keys, values):
    arrays = (queries, keys, values)
    rows = KV_ROWS + Q_ROWS
    extra = packed(pack_extra_kernel, arrays, [(rows, PAIR)] * 4, EXTRA * HEAD_DIM, 60)
    (sent,) = packed(pack_main_kernel, arrays, [(COLUMNS, rows, PAIR)], COLUMNS * HEAD_DIM, 12)

    extra = [extra[0]] + [along("x", a, step) for a, step in zip(extra[1:], STEPS, strict=True)]
    xkv, xq = gather(extra)
    xqs = [xq] + [along("y", xq, step) for step in STEPS]
    xkvs = [xkv, along_z(xkv, 1), along_z(xkv, 3)]
    xkvs.append(along_z(xkvs[1], 1))

    got = lax.all_to_all(sent, ("x", "y"), 0, 0, tiled=True)
    kv, q = sort(got)
    near = key_partner(kv)
    near_q = query_partner(q)
    both = stack(kv, *xkvs)
    other = other_core(both)

    rows = kv.shape[0]
    own = attend(q, [kv, other[:rows]], None, None)
    xq = stack(*xqs, flops=2 * 10**10)
    parts = attend(xq, [both[rows:], other[rows:]], None, "part", own[:1])

    near = hold(near, parts[0], near_q)
    near_other = other_core(near)
    state = attend(near_q, [kv, other[:rows]], None, None, (near,))
    sent = attend(near_q, [near, near_other], state, "send")
    back = [along("y", part, -step) for part, step in zip(parts[1:], STEPS, strict=True)]
    own = attend(q, [near, near_other], own, None, (sent,))
    out = merge(*own, query_partner(sent), *back)
    xout = combine([parts[0], *back])
    out = lax.all_to_all(out.reshape(COLUMNS, Q_ROWS, PAIR), ("x", "y"), 0, 0, tiled=True)
    xout = [xout[0]] + [along("x", a, -step) for a, step in zip(xout[1:], STEPS, strict=True)]
    return unpack(out, xout)


def solution(mesh):
    fine = Mesh(mesh.devices.reshape(SIZES), AXES)
    return jax.shard_map(
        local, mesh=fine, in_specs=(P(AXES, None),) * 3, out_specs=P(AXES, None), check_vma=False
    )
```

```python
import functools

import jax
import jax.numpy as jnp
from jax import lax
from jax.experimental import pallas as pl
from jax.experimental.pallas import tpu as pltpu
from jax.sharding import Mesh, PartitionSpec as P

HEADS = 20
HEAD_DIM = 128
PAIR = 2 * HEAD_DIM
SCALE = HEAD_DIM**-0.5 * 1.4426950408889634
AXES = ("x", "zl", "y", "zh", "c")
SIZES = (4, 2, 4, 2, 2)
COLUMNS = 16
TOKENS = 80
EXTRA = HEADS - COLUMNS
K_BLOCK = 256
CODE_ROWS = 16
STEPS = (1, 3, 2)
NT = (((1,), (1,)), ((), ()))
KV_ROWS, Q_ROWS = TOKENS, TOKENS // 2
VMEM = pl.BlockSpec(memory_space=pltpu.VMEM)
HBM = pl.BlockSpec(memory_space=pltpu.HBM)


def along_z(a, step):
    pairs = []
    for zl in range(2):
        for zh in range(2):
            z = (2 * zh + zl + step) % 4
            pairs.append((2 * zl + zh, 2 * (z % 2) + z // 2))
    return lax.ppermute(a, ("zl", "zh"), pairs)


def along(axis, a, step):
    return lax.ppermute(a, axis, [(i, (i + step) % 4) for i in range(4)])


def key_partner(a):
    return lax.ppermute(a, "zl", [(0, 1), (1, 0)])


def query_partner(a):
    return lax.ppermute(a, ("zl", "zh"), [(0, 3), (3, 0), (1, 2), (2, 1)])


def other_core(a):
    return lax.ppermute(a, "c", [(0, 1), (1, 0)])


def scaled_halves(q):
    full = q.astype(jnp.float32) * SCALE
    high = full.astype(jnp.bfloat16)
    low = (full - high.astype(jnp.float32)).astype(jnp.bfloat16)
    return jnp.concatenate([high, low], axis=1)


def diagonal():
    shape = (HEAD_DIM, HEAD_DIM)
    return lax.broadcasted_iota(jnp.int32, shape, 0) == lax.broadcasted_iota(jnp.int32, shape, 1)


def coded_rows(level):
    blocks = level.shape[0] // HEAD_DIM
    row = lax.broadcasted_iota(jnp.int32, (CODE_ROWS, HEAD_DIM), 0)
    coded = jnp.zeros((CODE_ROWS, HEAD_DIM), jnp.float32)
    for i in range(blocks):
        block = jnp.where(diagonal(), level[i * HEAD_DIM : (i + 1) * HEAD_DIM, :], 0.0)
        rest = jnp.sum(block, axis=0, keepdims=True)
        for term in range(3):
            rounded = rest.astype(jnp.bfloat16).astype(jnp.float32)
            coded = jnp.where(row == term * blocks + i, rounded, coded)
            rest = rest - rounded
    return coded


def decoded_column(coded, i, blocks):
    row = lax.broadcasted_iota(jnp.int32, coded.shape, 0)
    mine = (row == i) | (row == blocks + i) | (row == 2 * blocks + i)
    numbers = jnp.sum(jnp.where(mine, coded, 0.0), axis=0, keepdims=True)
    return jnp.sum(jnp.where(diagonal(), numbers, 0.0), axis=1, keepdims=True)


def attend_kernel(n_kv, n_after, first, last, *refs):
    refs = list(refs)
    q_ref, kv_refs, refs = refs[0], refs[1 : 1 + n_kv], refs[1 + n_kv :]
    if not first:
        acc_in, top_in = refs[:2]
        refs = refs[2:]
    refs = refs[n_after:]
    rows = q_ref.shape[0]
    ones = jnp.ones((K_BLOCK, HEAD_DIM), jnp.bfloat16)
    q = jnp.concatenate([scaled_halves(q_ref[:, :HEAD_DIM]), scaled_halves(q_ref[:, HEAD_DIM:])], axis=0)
    if first:
        top = jnp.full((2 * rows, 1), -1e30, jnp.float32)
        acc = jnp.zeros((2 * rows, PAIR), jnp.float32)
    else:
        top = jnp.max(top_in[...], axis=1, keepdims=True)
        acc = acc_in[...]
    for kv_ref in kv_refs:
        for j in range(kv_ref.shape[0] // K_BLOCK):
            there = slice(j * K_BLOCK, (j + 1) * K_BLOCK)
            k = kv_ref[there, :HEAD_DIM]
            v = kv_ref[there, HEAD_DIM:]
            scores = lax.dot_general(
                q, jnp.concatenate([k, k], axis=1), NT, preferred_element_type=jnp.float32
            )
            fresh = jnp.maximum(top, jnp.max(scores, axis=1, keepdims=True))
            weights = jnp.exp2(scores - fresh).astype(jnp.bfloat16)
            acc = acc * jnp.exp2(top - fresh) + jnp.dot(
                weights, jnp.concatenate([v, ones], axis=1), preferred_element_type=jnp.float32
            )
            top = fresh
    whole_top, whole_acc = top, acc
    for half in range(2):
        lanes = slice(half * HEAD_DIM, (half + 1) * HEAD_DIM)
        here = slice(half * rows, (half + 1) * rows)
        top, acc = whole_top[here, :], whole_acc[here, :]
        if last == "send":
            total = acc[:, HEAD_DIM:]
            refs[0][:rows, lanes] = (acc[:, :HEAD_DIM] / total).astype(jnp.bfloat16)
            refs[0][rows:, lanes] = coded_rows(top + jnp.log2(total)).astype(jnp.bfloat16)
        elif last == "part":
            total = acc[:, HEAD_DIM:]
            part = (acc[:, :HEAD_DIM] / total).astype(jnp.bfloat16)
            coded = coded_rows(top + jnp.log2(total)).astype(jnp.bfloat16)
            some = rows // 4
            for i, ref in enumerate(refs):
                ref[:some, lanes] = part[i * some : (i + 1) * some, :]
                ref[some:, lanes] = coded
        else:
            refs[0][here, :] = acc
            refs[1][here, :] = jnp.broadcast_to(top, (rows, HEAD_DIM))


def attend(q, kvs, state, last, after=(), flops=0):
    rows = q.shape[0]
    keys = sum(kv.shape[0] for kv in kvs)
    if last is None:
        out_shape = (
            jax.ShapeDtypeStruct((2 * rows, PAIR), jnp.float32),
            jax.ShapeDtypeStruct((2 * rows, HEAD_DIM), jnp.float32),
        )
    elif last == "part":
        out_shape = (jax.ShapeDtypeStruct((rows // 4 + CODE_ROWS, PAIR), jnp.bfloat16),) * 4
    else:
        out_shape = (jax.ShapeDtypeStruct((rows + CODE_ROWS, PAIR), jnp.bfloat16),)
    args = (q, *kvs, *(state or ()))
    result = pl.pallas_call(
        functools.partial(attend_kernel, len(kvs), len(after), state is None, last),
        out_shape=out_shape,
        in_specs=[VMEM] * len(args) + [HBM] * len(after),
        out_specs=(VMEM,) * len(out_shape),
        compiler_params=pltpu.CompilerParams(vmem_limit_bytes=20 * 2**20),
        cost_estimate=pl.CostEstimate(
            flops=flops, bytes_accessed=4 * keys * HEAD_DIM, transcendentals=0
        ),
    )(*args, *after)
    return result[0] if last == "send" else result


def combine_kernel(*refs):
    parts, outs = refs[:4], refs[4:]
    rows = parts[0].shape[0] - CODE_ROWS
    blocks = 4 * rows // HEAD_DIM
    for half in range(2):
        lanes = slice(half * HEAD_DIM, (half + 1) * HEAD_DIM)
        levels = []
        for i, part in enumerate(parts):
            first, start = divmod(i * rows, HEAD_DIM)
            coded = part[rows:, lanes].astype(jnp.float32)
            column = jnp.concatenate([decoded_column(coded, first + j, blocks) for j in range(2)], axis=0)
            levels.append(column[start : start + rows, :])
        top = functools.reduce(jnp.maximum, levels)
        shares = [jnp.exp2(level - top) for level in levels]
        total = functools.reduce(jnp.add, shares)
        summed = functools.reduce(
            jnp.add, [share * p[:rows, lanes].astype(jnp.float32) for share, p in zip(shares, parts, strict=True)]
        )
        whole = (summed / total).astype(jnp.bfloat16)
        for i, out in enumerate(outs):
            out[:, lanes] = whole[i * Q_ROWS : (i + 1) * Q_ROWS, :]


def combine(parts):
    rows = parts[0].shape[0]
    return pl.pallas_call(
        combine_kernel,
        out_shape=[jax.ShapeDtypeStruct((Q_ROWS, PAIR), jnp.bfloat16)] * 4,
        in_specs=[VMEM] * 4,
        out_specs=[VMEM] * 4,
        compiler_params=pltpu.CompilerParams(vmem_limit_bytes=8 * 2**20),
        cost_estimate=pl.CostEstimate(flops=16 * rows * PAIR, bytes_accessed=16 * rows * PAIR, transcendentals=0),
    )(*parts)


def fetch(sources, first, scratch, sems):
    copies = [
        pltpu.make_async_copy(source.at[:, pl.ds(first, held.shape[1])], held, sems.at[i])
        for i, (source, held) in enumerate(zip(sources, scratch, strict=True))
    ]
    for copy in copies:
        copy.start()
    for copy in copies:
        copy.wait()


def pack(out, q_ref, k_ref, v_ref, lanes):
    out[:KV_ROWS, :HEAD_DIM] = k_ref[:, lanes]
    out[:KV_ROWS, HEAD_DIM:] = v_ref[:, lanes]
    out[KV_ROWS:, :HEAD_DIM] = q_ref[:Q_ROWS, lanes]
    out[KV_ROWS:, HEAD_DIM:] = q_ref[Q_ROWS:, lanes]


def pack_extra_kernel(*refs):
    sources, outs, scratch, sems = refs[:3], refs[3:7], refs[7:10], refs[10]
    fetch(sources, COLUMNS * HEAD_DIM, scratch, sems)
    x = lax.axis_index("x")
    for step, out in zip((0, *STEPS), outs, strict=True):
        head = lax.rem(x + step, 4)
        pack(out, *scratch, pl.ds(pl.multiple_of(head * HEAD_DIM, HEAD_DIM), HEAD_DIM))


def pack_main_kernel(*refs):
    sources, out, scratch, sems = refs[:3], refs[3], refs[4:7], refs[7]
    fetch(sources, 0, scratch, sems)
    for head in range(COLUMNS):
        pack(out.at[head], *scratch, pl.ds(head * HEAD_DIM, HEAD_DIM))


def packed(kernel, arrays, shapes, columns, grant):
    return pl.pallas_call(
        kernel,
        out_shape=[jax.ShapeDtypeStruct(shape, jnp.bfloat16) for shape in shapes],
        in_specs=[HBM] * 3,
        out_specs=[VMEM] * len(shapes),
        scratch_shapes=[pltpu.VMEM((TOKENS, columns), jnp.bfloat16)] * 3 + [pltpu.SemaphoreType.DMA((3,))],
        compiler_params=pltpu.CompilerParams(vmem_limit_bytes=grant * 2**20),
        cost_estimate=pl.CostEstimate(flops=0, bytes_accessed=2**20, transcendentals=0),
    )(*arrays)


def gather_kernel(*refs):
    pieces, xkv, xq = refs[:4], refs[4], refs[5]
    for i, piece in enumerate(pieces):
        xkv[i * KV_ROWS : (i + 1) * KV_ROWS, :] = piece[:KV_ROWS, :]
        xq[i * Q_ROWS : (i + 1) * Q_ROWS, :] = piece[KV_ROWS:, :]


def gather(pieces):
    return pl.pallas_call(
        gather_kernel,
        out_shape=[jax.ShapeDtypeStruct((4 * rows, PAIR), jnp.bfloat16) for rows in (KV_ROWS, Q_ROWS)],
        in_specs=[VMEM] * 4,
        out_specs=[VMEM] * 2,
        compiler_params=pltpu.CompilerParams(vmem_limit_bytes=8 * 2**20),
        cost_estimate=pl.CostEstimate(flops=2 * 10**10, bytes_accessed=2**20, transcendentals=0),
    )(*pieces)


def sort_kernel(got, kv, q):
    for i in range(COLUMNS):
        kv[i * KV_ROWS : (i + 1) * KV_ROWS, :] = got[i, :KV_ROWS, :]
        q[i * Q_ROWS : (i + 1) * Q_ROWS, :] = got[i, KV_ROWS:, :]


def sort(got):
    return pl.pallas_call(
        sort_kernel,
        out_shape=[jax.ShapeDtypeStruct((COLUMNS * rows, PAIR), jnp.bfloat16) for rows in (KV_ROWS, Q_ROWS)],
        in_specs=[VMEM],
        out_specs=[VMEM] * 2,
        compiler_params=pltpu.CompilerParams(vmem_limit_bytes=12 * 2**20),
        cost_estimate=pl.CostEstimate(flops=0, bytes_accessed=2**20, transcendentals=0),
    )(got)


def stack_kernel(*refs):
    out, start = refs[-1], 0
    for ref in refs[:-1]:
        if start < out.shape[0]:
            out[start : start + ref.shape[0], :] = ref[...]
            start += ref.shape[0]


def stack(*pieces, after=(), flops=0):
    return pl.pallas_call(
        stack_kernel,
        out_shape=jax.ShapeDtypeStruct((sum(piece.shape[0] for piece in pieces), PAIR), jnp.bfloat16),
        in_specs=[VMEM] * len(pieces) + [HBM] * len(after),
        out_specs=VMEM,
        compiler_params=pltpu.CompilerParams(vmem_limit_bytes=12 * 2**20),
        cost_estimate=pl.CostEstimate(flops=flops, bytes_accessed=2**20, transcendentals=0),
    )(*pieces, *after)


def hold_kernel(a, *refs):
    refs[-1][...] = a[...]


def hold(a, *after):
    return pl.pallas_call(
        hold_kernel,
        out_shape=jax.ShapeDtypeStruct(a.shape, a.dtype),
        in_specs=[VMEM] + [HBM] * len(after),
        out_specs=VMEM,
        compiler_params=pltpu.CompilerParams(vmem_limit_bytes=12 * 2**20),
        cost_estimate=pl.CostEstimate(flops=0, bytes_accessed=2**20, transcendentals=0),
    )(a, *after)


def merge_kernel(acc, top, sent, *refs):
    out = refs[-1]
    rows = out.shape[0]
    blocks = rows // HEAD_DIM
    for half in range(2):
        lanes = slice(half * HEAD_DIM, (half + 1) * HEAD_DIM)
        coded = sent[rows:, lanes].astype(jnp.float32)
        for i in range(blocks):
            there = slice(i * HEAD_DIM, (i + 1) * HEAD_DIM)
            here = slice(half * rows + i * HEAD_DIM, half * rows + (i + 1) * HEAD_DIM)
            other = decoded_column(coded, i, blocks)
            largest = jnp.maximum(top[here, :], other)
            share, other = jnp.exp2(top[here, :] - largest), jnp.exp2(other - largest)
            summed = acc[here, :HEAD_DIM] * share + sent[there, lanes].astype(jnp.float32) * other
            out[there, lanes] = (summed / (acc[here, HEAD_DIM:] * share + other)).astype(jnp.bfloat16)


def merge(acc, top, sent, *after):
    return pl.pallas_call(
        merge_kernel,
        out_shape=jax.ShapeDtypeStruct((acc.shape[0] // 2, PAIR), jnp.bfloat16),
        in_specs=[VMEM] * 3 + [HBM] * len(after),
        out_specs=VMEM,
        compiler_params=pltpu.CompilerParams(vmem_limit_bytes=12 * 2**20),
        cost_estimate=pl.CostEstimate(flops=0, bytes_accessed=2**20, transcendentals=0),
    )(acc, top, sent, *after)


def unpack_kernel(main, *refs):
    extra, out = refs[:4], refs[4]

    def put(block, lanes):
        out[:Q_ROWS, lanes] = block[:, :HEAD_DIM]
        out[Q_ROWS:, lanes] = block[:, HEAD_DIM:]

    for head in range(COLUMNS):
        put(main.at[head], pl.ds(head * HEAD_DIM, HEAD_DIM))
    x = lax.axis_index("x")
    for step, block in zip((0, *STEPS), extra, strict=True):
        head = COLUMNS + lax.rem(x + step, 4)
        put(block, pl.ds(pl.multiple_of(head * HEAD_DIM, HEAD_DIM), HEAD_DIM))


def unpack(main, extra):
    return pl.pallas_call(
        unpack_kernel,
        out_shape=jax.ShapeDtypeStruct((TOKENS, HEADS * HEAD_DIM), jnp.bfloat16),
        in_specs=[VMEM] * 5,
        out_specs=VMEM,
        compiler_params=pltpu.CompilerParams(vmem_limit_bytes=8 * 2**20),
        cost_estimate=pl.CostEstimate(flops=0, bytes_accessed=2**20, transcendentals=0),
    )(main, *extra)


def local(queries, keys, values):
    arrays = (queries, keys, values)
    rows = KV_ROWS + Q_ROWS
    extra = packed(pack_extra_kernel, arrays, [(rows, PAIR)] * 4, EXTRA * HEAD_DIM, 60)
    (sent,) = packed(pack_main_kernel, arrays, [(COLUMNS, rows, PAIR)], COLUMNS * HEAD_DIM, 12)

    extra = [extra[0]] + [along("x", a, step) for a, step in zip(extra[1:], STEPS, strict=True)]
    xkv, xq = gather(extra)
    xqs = [xq] + [along("y", xq, step) for step in STEPS]
    xkvs = [xkv] + [along_z(xkv, step) for step in STEPS]

    got = lax.all_to_all(sent, ("x", "y"), 0, 0, tiled=True)
    kv, q = sort(got)
    near = key_partner(kv)
    near_q = query_partner(q)
    both = stack(kv, *xkvs)
    other = other_core(both)

    rows = kv.shape[0]
    own = attend(q, [kv, other[:rows]], None, None)
    xq = stack(*xqs, flops=2 * 10**10)
    parts = attend(xq, [both[rows:], other[rows:]], None, "part", own[:1])

    near = hold(near, parts[0], near_q)
    near_other = other_core(near)
    state = attend(near_q, [kv, other[:rows]], None, None, (near,))
    sent = attend(near_q, [near, near_other], state, "send")
    back = [along("y", part, -step) for part, step in zip(parts[1:], STEPS, strict=True)]
    own = attend(q, [near, near_other], own, None, (sent,))
    out = merge(*own, query_partner(sent), *back)
    xout = combine([parts[0], *back])
    out = lax.all_to_all(out.reshape(COLUMNS, Q_ROWS, PAIR), ("x", "y"), 0, 0, tiled=True)
    xout = [xout[0]] + [along("x", a, -step) for a, step in zip(xout[1:], STEPS, strict=True)]
    return unpack(out, xout)


def solution(mesh):
    fine = Mesh(mesh.devices.reshape(SIZES), AXES)
    return jax.shard_map(
        local, mesh=fine, in_specs=(P(AXES, None),) * 3, out_specs=P(AXES, None), check_vma=False
    )
```
